32 devices in a mesh: groups: 2 (over x), seq: 8 (over z, y), head: 2 (over core).
Axes of the slice: x: 2, y: 2, z: 4, core: 2. Of those that a mesh axis runs over, the one named last changes fastest.
Arguments:
- query_rows: bfloat16 [2048, 6144], P(('groups', 'seq'), 'head'), parts along dimension 0
- key_rows: bfloat16 [2048, 6144], P(('groups', 'seq'), 'head'), parts along dimension 0, may hold values from -6 to 6
- value_rows: bfloat16 [2048, 6144], P(('groups', 'seq'), 'head'), parts along dimension 0, may hold values from -6 to 6
- key_len: int32 [16], P('groups'), parts along dimension 0, may hold values from 2 to 128, as said below
- linear_scale: float32 [48], P('head'), may hold values from 0.5 to 2
Outputs:
- attended: bfloat16 [2048, 6144], P(('groups', 'seq'), 'head'), parts along dimension 0
The draws below stay inside these ranges and needn't reach their ends.
There are 2 independent parts, one for each index of `groups`. The reference program is written for one: setup_inputs(seed, part) draws one part's arguments, and reference() takes and returns one part's arrays. A program takes and returns all parts, laid end to end along the dimension named above; an argument that names none is the same for every part. Nothing has to cross between parts.
Inputs may be any that keep to these rules, and one draw needn't show every extreme that they name: `key_len`: one block has exactly 128 valid keys in every draw.
All inputs are finite; a program needn't handle non-finite values.
Results may differ from the reference program's by a relative error of at most 0.00135.
Values may be sent and summed in bfloat16 or wider, within the bound.
No kernel may reach another device: no remote copies, remote signals or barrier semaphores. Data moves between devices by JAX's collectives and lax.ppermute only.
A program may use at most 256 MiB of HBM per device.

```python
import math
import jax
import jax.numpy as jnp
from jax import lax

HD = 128
HEADS = 48
BLOCK = 128
TOKENS = 1024


def base_keys(key):
    source = jax.random.fold_in(key, 11)
    drawn = jax.random.truncated_normal(source, -6.0, 6.0, (TOKENS, HEADS * HD), jnp.float32)
    return drawn


def draw_key_rows(key, part):
    return base_keys(key).astype(jnp.bfloat16)


def draw_query_rows(key, part):
    source = jax.random.fold_in(key, 12)
    drawn = 3.0 * jax.random.truncated_normal(source, -6.0, 6.0, (TOKENS, HEADS * HD), jnp.float32)
    return drawn.astype(jnp.bfloat16)


def draw_key_len(key, part):
    block_count = TOKENS // BLOCK
    lengths = jax.random.randint(jax.random.fold_in(key, 21), (block_count,), 2, BLOCK + 1, dtype=jnp.int32)
    chosen = jax.random.randint(jax.random.fold_in(key, 22), (), 0, block_count, dtype=jnp.int32)
    return lengths.at[chosen].set(BLOCK)


def steps_of(own_key, extent, cuts, least, high):
    gain, own = 1.0, jax.random.fold_in(own_key, 6)
    for dim, blocks in cuts:
        heights = jnp.exp(jax.random.uniform(jax.random.fold_in(own, dim), (blocks,), jnp.float32, least / len(cuts), high / len(cuts)))
        gain = gain * jnp.repeat(heights, extent[dim] // blocks).reshape([-1 if axis == dim else 1 for axis in range(len(extent))])
    return gain


def noise(own_key, dims, width, most, cuts=(), kind=jnp.bfloat16):
    loudness = steps_of(own_key, dims, cuts, -0.22, 0.18) if cuts else 1.0
    array = jax.random.normal(own_key, dims, jnp.float32) * width * loudness
    return jnp.minimum(jnp.maximum(array, -most), most).astype(kind)


def setup_inputs(seed: int = 0, part: int = 0) -> dict:
    key_list = jax.random.split(jax.random.key(seed), 6)
    part_keys = jax.random.split(jax.random.fold_in(key_list[5], part), 6)
    return {
        "query_rows": draw_query_rows(jax.random.fold_in(jax.random.fold_in(key_list[5], part), 71), part),
        "key_rows": draw_key_rows(jax.random.fold_in(jax.random.fold_in(key_list[5], part), 71), part),
        "value_rows": noise(part_keys[2], (TOKENS, HEADS * HD), 1.0, 6.0, ((0, 8), (1, 2))),
        "key_len": draw_key_len(jax.random.fold_in(jax.random.fold_in(key_list[5], part), 71), part),
        "linear_scale": jnp.clip(jnp.exp(math.log(2.0) - 1.3862944 * jax.random.uniform(key_list[4], (HEADS,), jnp.float32) ** steps_of(key_list[4], (HEADS,), ((0, 2),), -0.2, 0.2)), 0.5, 2.0),
    }


def feature(inputs):
    return jnp.where(inputs > 0.0, inputs + 1.0, jnp.exp(jnp.minimum(inputs, 0.0)))

def partial_block(query_block, key_block, value_block, live_count, causal):
    scores = jnp.einsum('rhd,chd->hrc', query_block.astype(jnp.float32), key_block.astype(jnp.float32), precision=lax.Precision.HIGHEST) * (1.0 / math.sqrt(HD))
    columns = lax.broadcasted_iota(jnp.int32, scores.shape, 2)
    allowed = columns < live_count
    if causal:
        allowed = allowed & (columns <= lax.broadcasted_iota(jnp.int32, scores.shape, 1))
    row_peak = lax.optimization_barrier(jnp.max(jnp.where(allowed, scores, -jnp.inf), axis=2))
    weights = jnp.where(allowed, jnp.exp(scores - row_peak[:, :, None]), 0.0).astype(jnp.bfloat16)
    row_total = lax.optimization_barrier(jnp.sum(weights.astype(jnp.float32), axis=2))
    numerator = jnp.einsum('hrc,chd->rhd', weights.astype(jnp.float32), value_block.astype(jnp.float32), precision=lax.Precision.HIGHEST)
    return (numerator, row_peak, row_total)

def combine(pieces):
    row_peak = pieces[0][1]
    for one_piece in pieces[1:]:
        row_peak = jnp.maximum(row_peak, one_piece[1])
    numerator = jnp.zeros_like(pieces[0][0])
    denominator = jnp.zeros_like(pieces[0][2])
    for one_piece in pieces:
        factor = jnp.exp(one_piece[1] - row_peak)
        numerator = numerator + jnp.transpose(factor)[:, :, None] * one_piece[0]
        denominator = denominator + factor * one_piece[2]
    return numerator / jnp.transpose(denominator)[:, :, None]

def reference(query_rows, key_rows, value_rows, key_len, linear_scale):
    blocks = TOKENS // BLOCK
    levels = blocks.bit_length() - 1
    queries = query_rows.reshape(blocks, BLOCK, HEADS, HD)
    key_heads = key_rows.reshape(blocks, BLOCK, HEADS, HD)
    value_heads = value_rows.reshape(blocks, BLOCK, HEADS, HD)

    def block_sum(inputs):
        key_block, value_block, live_count = inputs
        live_rows = (jnp.arange(BLOCK, dtype=jnp.int32) < live_count)[:, None, None]
        mapped = jnp.where(live_rows, feature(key_block.astype(jnp.float32)), 0.0)
        return jnp.einsum('rhd,rhe->hde', mapped, value_block.astype(jnp.float32), precision=lax.Precision.HIGHEST)
    all_sums = lax.map(block_sum, (key_heads, value_heads, key_len))
    prefix = jnp.concatenate([jnp.zeros_like(all_sums[:1]), jnp.cumsum(all_sums[:-1], axis=0)], axis=0)

    def one_block(inputs):
        query_block, prefix_block, block_id = inputs
        pieces = [partial_block(query_block, key_heads[block_id], value_heads[block_id], key_len[block_id], True)]
        for bit_level in range(levels):
            partner = jnp.bitwise_xor(block_id, 1 << bit_level).astype(jnp.int32)
            pieces.append(partial_block(query_block, key_heads[partner], value_heads[partner], key_len[partner], False))
        attention = combine(pieces)
        linear = jnp.einsum('rhd,hde->rhe', feature(query_block.astype(jnp.float32)), prefix_block, precision=lax.Precision.HIGHEST)
        linear = linear * (linear_scale[None, :, None] / (HD * math.sqrt(TOKENS)))
        return (attention + linear).astype(jnp.bfloat16)
    output = lax.map(one_block, (queries, prefix, jnp.arange(blocks, dtype=jnp.int32)))
    return output.reshape(TOKENS, HEADS * HD)
```

```python
import functools
import math

import jax
import jax.numpy as jnp
from jax import lax
from jax.experimental import pallas as pl
from jax.experimental.pallas import tpu as pltpu
from jax.sharding import PartitionSpec as P

CENTER = 1.125
TERMS = 3
HEADS_A_STEP = 4
VMEM_BYTES = 40 * 1024 * 1024
F32 = jnp.float32
BF16 = jnp.bfloat16


def feature(x):
    return jnp.where(x > 0.0, x + 1.0, jnp.exp(jnp.minimum(x, 0.0)))


def halves(x):
    high = x.astype(BF16)
    return high, (x - high.astype(F32)).astype(BF16)


def padded(count):
    return -(-count // 16) * 16


def store_packed(ref, main, sums):
    rows, extra = main.shape[0], sums.shape[0]
    ref[0:rows, :] = main.astype(BF16)
    for term in range(TERMS):
        part = sums.astype(BF16)
        sums = sums - part.astype(F32)
        ref[rows + term * extra : rows + (term + 1) * extra, :] = part


def packed_sums(ref, rows, extra):
    total = ref[rows : rows + extra, :].astype(F32)
    for term in range(1, TERMS):
        total = total + ref[rows + term * extra : rows + (term + 1) * extra, :].astype(F32)
    return total


def block_sums_kernel(heads, width, where, lengths, k_ref, v_ref, send_ref, keep_ref):
    half_heads = heads // 2
    me = where[0]
    side = lax.rem(me, 2)
    length = lengths[me]
    rows = half_heads * width
    extra = padded(half_heads)
    live = lax.broadcasted_iota(jnp.int32, (k_ref.shape[0], width), 0) < length

    def one_half(first, store):
        sums = []
        for i in range(half_heads):
            columns = pl.ds(pl.multiple_of((first + i) * width, width), width)
            mapped = jnp.where(live, feature(k_ref[:, columns].astype(F32)) - CENTER, 0.0)
            values = jnp.where(live, v_ref[:, columns].astype(F32), 0.0)
            sums.append(jnp.sum(values, axis=0, keepdims=True))
            high, low = halves(mapped)
            values = values.astype(BF16)
            store(
                i,
                lax.dot_general(
                    jnp.concatenate([high, low], axis=0),
                    jnp.concatenate([values, values], axis=0),
                    (((0,), (0,)), ((), ())),
                    preferred_element_type=F32,
                ),
            )
        sums += [jnp.zeros((1, width), F32)] * (extra - half_heads)
        return jnp.concatenate(sums, axis=0)

    def store_send(i, value):
        send_ref[i * width : (i + 1) * width, :] = value.astype(BF16)

    def store_keep(i, value):
        keep_ref[i * width : (i + 1) * width, :] = value

    sums = one_half((1 - side) * half_heads, store_send)
    for term in range(TERMS):
        part = sums.astype(BF16)
        sums = sums - part.astype(F32)
        send_ref[rows + term * extra : rows + (term + 1) * extra, :] = part
    keep_ref[rows : rows + extra, :] = one_half(side * half_heads, store_keep)


def add_packed_kernel(rows, extra, count, where, keep_ref, *refs):
    flag = where[0].astype(F32)
    main = keep_ref[0:rows, :] * flag
    sums = keep_ref[rows : rows + extra, :] * flag
    for ref in refs[:count]:
        main = main + ref[0:rows, :].astype(F32)
        sums = sums + packed_sums(ref, rows, extra)
    store_packed(refs[count], main, sums)


def scores_kernel(heads, width, levels, hops, tokens, where, lengths, scale, *refs):
    step = pl.program_id(0)
    refs = list(refs)
    q_ref = refs.pop(0)
    key_refs = [refs.pop(0) for _ in range(levels + 1)]
    value_refs = [refs.pop(0) for _ in range(2)]
    hop_refs = [refs.pop(0) for _ in range(hops)]
    near_ref, far_ref = refs.pop(0), refs.pop(0)
    weight_refs = [refs.pop(0) for _ in range(levels - 1)]
    factor_ref, base_ref = refs
    me = where[0]
    side = lax.rem(me, 2)
    half_heads = heads // 2
    rows, extra = half_heads * width, padded(half_heads)
    row_count = q_ref.shape[0]
    a_step = q_ref.shape[1] // width
    first = step * a_step
    column = lax.broadcasted_iota(jnp.int32, (row_count, row_count), 1)
    row = lax.broadcasted_iota(jnp.int32, (row_count, row_count), 0)
    allowed = []
    for which in range(levels + 1):
        partner = me if which == 0 else jnp.bitwise_xor(me, 1 << (which - 1))
        fits = column < lengths[partner]
        allowed.append(fits & (column <= row) if which == 0 else fits)
    lane = lax.broadcasted_iota(jnp.int32, (row_count, 128), 1)
    factors = jnp.zeros((row_count, 128), F32)
    mine = (first // half_heads == side).astype(F32)
    upper = mine * side.astype(F32)
    in_half = lax.rem(first, half_heads)
    sums = (1.0 - mine) * packed_sums(far_ref, rows, extra) + upper * packed_sums(near_ref, rows, extra)
    for ref in hop_refs:
        sums = sums + mine * packed_sums(ref, rows, extra)
    sum_row = lax.broadcasted_iota(jnp.int32, sums.shape, 0)
    for h in range(a_step):
        at = slice(h * width, (h + 1) * width)
        queries = q_ref[:, at]
        peaks, totals, weights = [], [], []
        for which in range(levels + 1):
            s = lax.dot_general(
                queries, key_refs[which][:, at], (((1,), (1,)), ((), ())), preferred_element_type=F32
            ) * (1.0 / math.sqrt(width))
            s = jnp.where(allowed[which], s, -jnp.inf)
            peak = jnp.max(s, axis=1, keepdims=True)
            p = jnp.exp(s - peak).astype(BF16)
            peaks.append(peak)
            weights.append(p)
            totals.append(jnp.sum(p.astype(F32), axis=1, keepdims=True))
        peak = functools.reduce(jnp.maximum, peaks)
        shares = [jnp.exp(one - peak) for one in peaks]
        whole = functools.reduce(jnp.add, [a * b for a, b in zip(shares, totals)])
        shares = [share / whole for share in shares]
        base = shares[0] * jnp.dot(weights[0], value_refs[0][:, at], preferred_element_type=F32)
        base = base + shares[1] * jnp.dot(weights[1], value_refs[1][:, at], preferred_element_type=F32)
        for which in range(2, levels + 1):
            weight_refs[which - 2][:, at] = weights[which]
            factors = jnp.where(lane == (which - 2) * a_step + h, shares[which], factors)
        block = pl.ds(pl.multiple_of((in_half + h) * width, width), width)
        prefix = (1.0 - mine) * far_ref[block, :].astype(F32) + upper * near_ref[block, :].astype(F32)
        for ref in hop_refs:
            prefix = prefix + mine * ref[block, :].astype(F32)
        mapped = feature(queries.astype(F32))
        high, low = halves(mapped)
        prefix_high, prefix_low = halves(prefix)
        linear = jnp.dot(
            jnp.concatenate([high, low], axis=1),
            jnp.concatenate([prefix_high, prefix_high], axis=0),
            preferred_element_type=F32,
        ) + jnp.dot(high, prefix_low, preferred_element_type=F32)
        value_sum = jnp.sum(jnp.where(sum_row == in_half + h, sums, 0.0), axis=0, keepdims=True)
        linear = linear + jnp.sum(mapped, axis=1, keepdims=True) * (CENTER * value_sum)
        base_ref[:, at] = base + linear * (scale[first + h] * (1.0 / (width * math.sqrt(tokens))))
    factor_ref[...] = factors


def finish_kernel(late, width, factor_ref, base_ref, *refs):
    out_ref = refs[2 * late]
    a_step = base_ref.shape[1] // width
    for h in range(a_step):
        at = slice(h * width, (h + 1) * width)
        total = base_ref[:, at]
        for which in range(late):
            lane = which * a_step + h
            total = total + factor_ref[:, lane : lane + 1] * jnp.dot(
                refs[which][:, at], refs[late + which][:, at], preferred_element_type=F32
            )
        out_ref[:, at] = total.astype(BF16)


def params():
    return pltpu.CompilerParams(vmem_limit_bytes=VMEM_BYTES)


def shards(query_rows, key_rows, value_rows, key_len, linear_scale):
    row_count, columns = query_rows.shape
    heads = linear_scale.shape[0]
    width = columns // heads
    half_heads = heads // 2
    count = lax.axis_size("seq")
    levels = count.bit_length() - 1
    late = levels - 1
    me = lax.axis_index("seq").astype(jnp.int32)
    where = me.reshape(1)
    tokens = row_count * count
    rows, extra = half_heads * width, padded(half_heads)
    packed = jax.ShapeDtypeStruct((rows + TERMS * extra, width), BF16)
    smem = pl.BlockSpec(memory_space=pltpu.SMEM)
    vmem = pl.BlockSpec(memory_space=pltpu.VMEM)

    def swapped(x, level):
        return lax.ppermute(x, "seq", [(i, i ^ 1 << level) for i in range(count)])

    order = list(range(levels - 1, -1, -1))
    far_keys = {level: swapped(key_rows, level) for level in order}
    far_values = {level: swapped(value_rows, level) for level in order}

    send, keep = pl.pallas_call(
        functools.partial(block_sums_kernel, heads, width),
        in_specs=[smem, smem, vmem, vmem],
        out_specs=[vmem, vmem],
        out_shape=[packed, jax.ShapeDtypeStruct((rows + extra, width), F32)],
        compiler_params=params(),
        name="block_sums",
    )(where, key_len, key_rows, value_rows)
    near = swapped(send, 0)

    def add_packed(flag, *parts):
        return pl.pallas_call(
            functools.partial(add_packed_kernel, rows, extra, len(parts)),
            in_specs=[smem] + [vmem] * (1 + len(parts)),
            out_specs=vmem,
            out_shape=packed,
            compiler_params=params(),
            name="add_packed",
        )(flag, keep, *parts)

    one = jnp.ones((1,), jnp.int32)
    pairs_of_blocks = count // 2
    if pairs_of_blocks <= 4:
        steps = [[(z, z + 1)] for z in range(pairs_of_blocks - 1)]
    else:
        steps = [
            [(z, z + (1 << d)) for z in range(pairs_of_blocks - (1 << d))]
            for d in range((pairs_of_blocks - 1).bit_length())
        ]
    hops = []
    for pairs in steps:
        payload = add_packed(one, near, *hops)
        hops.append(
            lax.ppermute(payload, "seq", [(2 * a + y, 2 * b + y) for a, b in pairs for y in (0, 1)])
        )
    far = swapped(add_packed(1 - lax.rem(where, 2), *hops), 0)

    a_step = math.gcd(HEADS_A_STEP, half_heads)
    grid = (heads // a_step,)
    wide = pl.BlockSpec((row_count, a_step * width), lambda i, *_: (0, i))
    narrow = pl.BlockSpec((row_count, 128), lambda i, *_: (0, i))
    whole = pl.BlockSpec(packed.shape, lambda i, *_: (0, 0))
    full = jax.ShapeDtypeStruct((row_count, columns), BF16)
    *weights, factors, base = pl.pallas_call(
        functools.partial(scores_kernel, heads, width, levels, len(hops), tokens),
        grid_spec=pltpu.PrefetchScalarGridSpec(
            num_scalar_prefetch=3,
            grid=grid,
            in_specs=[wide] * (1 + levels + 1 + 2) + [whole] * (len(hops) + 2),
            out_specs=[wide] * late + [narrow, wide],
        ),
        out_shape=[full] * late
        + [
            jax.ShapeDtypeStruct((row_count, grid[0] * 128), F32),
            jax.ShapeDtypeStruct((row_count, columns), F32),
        ],
        compiler_params=params(),
        name="scores",
    )(
        where,
        key_len,
        linear_scale,
        query_rows,
        key_rows,
        *[far_keys[level] for level in range(levels)],
        value_rows,
        far_values[0],
        *hops,
        near,
        far,
    )
    return pl.pallas_call(
        functools.partial(finish_kernel, late, width),
        grid=grid,
        in_specs=[narrow, wide] + [wide] * (2 * late),
        out_specs=wide,
        out_shape=full,
        compiler_params=params(),
        name="finish",
    )(factors, base, *weights, *[far_values[level] for level in range(1, levels)])


def solution(mesh):
    return jax.shard_map(
        shards,
        mesh=mesh,
        in_specs=(
            P(("groups", "seq"), "head"),
            P(("groups", "seq"), "head"),
            P(("groups", "seq"), "head"),
            P("groups"),
            P("head"),
        ),
        out_specs=P(("groups", "seq"), "head"),
        check_vma=False,
    )
```

```python
import functools
import math

import jax
import jax.numpy as jnp
from jax import lax
from jax.experimental import pallas as pl
from jax.experimental.pallas import tpu as pltpu
from jax.sharding import PartitionSpec as P

CENTER = 1.125
TERMS = 3
HEADS_A_STEP = 4
VMEM_BYTES = 40 * 1024 * 1024
F32 = jnp.float32
BF16 = jnp.bfloat16


def feature(x):
    return jnp.where(x > 0.0, x + 1.0, jnp.exp(jnp.minimum(x, 0.0)))


def halves(x):
    high = x.astype(BF16)
    return high, (x - high.astype(F32)).astype(BF16)


def padded(count):
    return -(-count // 16) * 16


def store_packed(ref, main, sums):
    rows, extra = main.shape[0], sums.shape[0]
    ref[0:rows, :] = main.astype(BF16)
    for term in range(TERMS):
        part = sums.astype(BF16)
        sums = sums - part.astype(F32)
        ref[rows + term * extra : rows + (term + 1) * extra, :] = part


def packed_sums(ref, rows, extra):
    total = ref[rows : rows + extra, :].astype(F32)
    for term in range(1, TERMS):
        total = total + ref[rows + term * extra : rows + (term + 1) * extra, :].astype(F32)
    return total


def block_sums_kernel(heads, width, where, lengths, k_ref, v_ref, send_ref, keep_ref):
    half_heads = heads // 2
    me = where[0]
    side = lax.rem(me, 2)
    length = lengths[me]
    rows = half_heads * width
    extra = padded(half_heads)
    live = lax.broadcasted_iota(jnp.int32, (k_ref.shape[0], width), 0) < length

    def one_half(first, store):
        sums = []
        for i in range(half_heads):
            columns = pl.ds(pl.multiple_of((first + i) * width, width), width)
            mapped = jnp.where(live, feature(k_ref[:, columns].astype(F32)) - CENTER, 0.0)
            values = jnp.where(live, v_ref[:, columns].astype(F32), 0.0)
            sums.append(jnp.sum(values, axis=0, keepdims=True))
            high, low = halves(mapped)
            values = values.astype(BF16)
            store(
                i,
                lax.dot_general(
                    jnp.concatenate([high, low], axis=0),
                    jnp.concatenate([values, values], axis=0),
                    (((0,), (0,)), ((), ())),
                    preferred_element_type=F32,
                ),
            )
        sums += [jnp.zeros((1, width), F32)] * (extra - half_heads)
        return jnp.concatenate(sums, axis=0)

    def store_send(i, value):
        send_ref[i * width : (i + 1) * width, :] = value.astype(BF16)

    def store_keep(i, value):
        keep_ref[i * width : (i + 1) * width, :] = value

    sums = one_half((1 - side) * half_heads, store_send)
    for term in range(TERMS):
        part = sums.astype(BF16)
        sums = sums - part.astype(F32)
        send_ref[rows + term * extra : rows + (term + 1) * extra, :] = part
    keep_ref[rows : rows + extra, :] = one_half(side * half_heads, store_keep)


def add_packed_kernel(rows, extra, count, where, keep_ref, *refs):
    flag = where[0].astype(F32)
    main = keep_ref[0:rows, :] * flag
    sums = keep_ref[rows : rows + extra, :] * flag
    for ref in refs[:count]:
        main = main + ref[0:rows, :].astype(F32)
        sums = sums + packed_sums(ref, rows, extra)
    store_packed(refs[count], main, sums)


def scores_kernel(heads, width, levels, hops, tokens, where, lengths, scale, *refs):
    step = pl.program_id(0)
    refs = list(refs)
    q_ref = refs.pop(0)
    key_refs = [refs.pop(0) for _ in range(levels + 1)]
    value_refs = [refs.pop(0) for _ in range(2)]
    hop_refs = [refs.pop(0) for _ in range(hops)]
    near_ref, far_ref = refs.pop(0), refs.pop(0)
    weight_refs = [refs.pop(0) for _ in range(levels - 1)]
    factor_ref, base_ref = refs
    me = where[0]
    side = lax.rem(me, 2)
    half_heads = heads // 2
    rows, extra = half_heads * width, padded(half_heads)
    row_count = q_ref.shape[0]
    a_step = q_ref.shape[1] // width
    first = step * a_step
    column = lax.broadcasted_iota(jnp.int32, (row_count, row_count), 1)
    row = lax.broadcasted_iota(jnp.int32, (row_count, row_count), 0)
    allowed = []
    for which in range(levels + 1):
        partner = me if which == 0 else jnp.bitwise_xor(me, 1 << (which - 1))
        fits = column < lengths[partner]
        allowed.append(fits & (column <= row) if which == 0 else fits)
    lane = lax.broadcasted_iota(jnp.int32, (row_count, 128), 1)
    factors = jnp.zeros((row_count, 128), F32)
    mine = (first // half_heads == side).astype(F32)
    upper = mine * side.astype(F32)
    in_half = lax.rem(first, half_heads)
    sums = (1.0 - mine) * packed_sums(far_ref, rows, extra) + upper * packed_sums(near_ref, rows, extra)
    for ref in hop_refs:
        sums = sums + mine * packed_sums(ref, rows, extra)
    sum_row = lax.broadcasted_iota(jnp.int32, sums.shape, 0)
    for h in range(a_step):
        at = slice(h * width, (h + 1) * width)
        queries = q_ref[:, at]
        peaks, totals, weights = [], [], []
        for which in range(levels + 1):
            s = lax.dot_general(
                queries, key_refs[which][:, at], (((1,), (1,)), ((), ())), preferred_element_type=F32
            ) * (1.0 / math.sqrt(width))
            s = jnp.where(allowed[which], s, -jnp.inf)
            peak = jnp.max(s, axis=1, keepdims=True)
            p = jnp.exp(s - peak).astype(BF16)
            peaks.append(peak)
            weights.append(p)
            totals.append(jnp.sum(p.astype(F32), axis=1, keepdims=True))
        peak = functools.reduce(jnp.maximum, peaks)
        shares = [jnp.exp(one - peak) for one in peaks]
        whole = functools.reduce(jnp.add, [a * b for a, b in zip(shares, totals)])
        shares = [share / whole for share in shares]
        base = shares[0] * jnp.dot(weights[0], value_refs[0][:, at], preferred_element_type=F32)
        base = base + shares[1] * jnp.dot(weights[1], value_refs[1][:, at], preferred_element_type=F32)
        for which in range(2, levels + 1):
            weight_refs[which - 2][:, at] = weights[which]
            factors = jnp.where(lane == (which - 2) * a_step + h, shares[which], factors)
        block = pl.ds(pl.multiple_of((in_half + h) * width, width), width)
        prefix = (1.0 - mine) * far_ref[block, :].astype(F32) + upper * near_ref[block, :].astype(F32)
        for ref in hop_refs:
            prefix = prefix + mine * ref[block, :].astype(F32)
        mapped = feature(queries.astype(F32))
        high, low = halves(mapped)
        prefix_high, prefix_low = halves(prefix)
        linear = jnp.dot(
            jnp.concatenate([high, low], axis=1),
            jnp.concatenate([prefix_high, prefix_high], axis=0),
            preferred_element_type=F32,
        ) + jnp.dot(high, prefix_low, preferred_element_type=F32)
        value_sum = jnp.sum(jnp.where(sum_row == in_half + h, sums, 0.0), axis=0, keepdims=True)
        linear = linear + jnp.sum(mapped, axis=1, keepdims=True) * (CENTER * value_sum)
        base_ref[:, at] = base + linear * (scale[first + h] * (1.0 / (width * math.sqrt(tokens))))
    factor_ref[...] = factors


def finish_kernel(late, width, factor_ref, base_ref, *refs):
    out_ref = refs[2 * late]
    a_step = base_ref.shape[1] // width
    for h in range(a_step):
        at = slice(h * width, (h + 1) * width)
        total = base_ref[:, at]
        for which in range(late):
            lane = which * a_step + h
            total = total + factor_ref[:, lane : lane + 1] * jnp.dot(
                refs[which][:, at], refs[late + which][:, at], preferred_element_type=F32
            )
        out_ref[:, at] = total.astype(BF16)


def params():
    return pltpu.CompilerParams(vmem_limit_bytes=VMEM_BYTES)


def shards(query_rows, key_rows, value_rows, key_len, linear_scale):
    row_count, columns = query_rows.shape
    heads = linear_scale.shape[0]
    width = columns // heads
    half_heads = heads // 2
    count = lax.axis_size("seq")
    levels = count.bit_length() - 1
    late = levels - 1
    me = lax.axis_index("seq").astype(jnp.int32)
    where = me.reshape(1)
    tokens = row_count * count
    rows, extra = half_heads * width, padded(half_heads)
    packed = jax.ShapeDtypeStruct((rows + TERMS * extra, width), BF16)
    smem = pl.BlockSpec(memory_space=pltpu.SMEM)
    vmem = pl.BlockSpec(memory_space=pltpu.VMEM)

    def swapped(x, level):
        return lax.ppermute(x, "seq", [(i, i ^ 1 << level) for i in range(count)])

    order = list(range(levels - 1, 0, -1))
    far_keys = {level: swapped(key_rows, level) for level in order}
    neighbours = [[i, i + 1] for i in range(0, count, 2)]
    both_keys = lax.all_gather(key_rows, "seq", axis_index_groups=neighbours)
    both_values = lax.all_gather(value_rows, "seq", axis_index_groups=neighbours)
    far_values = {level: swapped(value_rows, level) for level in order}

    pairs_of_blocks = count // 2
    if pairs_of_blocks <= 4:
        steps = [[(z, z + 1)] for z in range(pairs_of_blocks - 1)]
    else:
        steps = [
            [(z, z + (1 << d)) for z in range(pairs_of_blocks - (1 << d))]
            for d in range((pairs_of_blocks - 1).bit_length())
        ]

    def prefix(where, key_len, key_rows, value_rows):
        send, keep = pl.pallas_call(
            functools.partial(block_sums_kernel, heads, width),
            in_specs=[smem, smem, vmem, vmem],
            out_specs=[vmem, vmem],
            out_shape=[packed, jax.ShapeDtypeStruct((rows + extra, width), F32)],
            compiler_params=params(),
            name="block_sums",
        )(where, key_len, key_rows, value_rows)
        near = swapped(send, 0)

        def add_packed(flag, *parts):
            return pl.pallas_call(
                functools.partial(add_packed_kernel, rows, extra, len(parts)),
                in_specs=[smem] + [vmem] * (1 + len(parts)),
                out_specs=vmem,
                out_shape=packed,
                compiler_params=params(),
                name="add_packed",
            )(flag, keep, *parts)

        one = jnp.ones((1,), jnp.int32)
        hops = []
        for pairs in steps:
            payload = add_packed(one, near, *hops)
            hops.append(
                lax.ppermute(payload, "seq", [(2 * a + y, 2 * b + y) for a, b in pairs for y in (0, 1)])
            )
        far = swapped(add_packed(1 - lax.rem(where, 2), *hops), 0)
        return near, far, *hops

    def nothing(*_):
        return tuple(jnp.zeros(packed.shape, packed.dtype) for _ in range(2 + len(steps)))

    near, far, *hops = lax.cond(key_len[0] > 0, prefix, nothing, where, key_len, key_rows, value_rows)

    a_step = math.gcd(HEADS_A_STEP, half_heads)
    grid = (heads // a_step,)
    wide = pl.BlockSpec((row_count, a_step * width), lambda i, *_: (0, i))
    paired = pl.BlockSpec(
        (None, row_count, a_step * width), lambda i, where, *_: (1 - lax.rem(where[0], 2), 0, i)
    )
    narrow = pl.BlockSpec((row_count, 128), lambda i, *_: (0, i))
    whole = pl.BlockSpec(packed.shape, lambda i, *_: (0, 0))
    full = jax.ShapeDtypeStruct((row_count, columns), BF16)
    *weights, factors, base = pl.pallas_call(
        functools.partial(scores_kernel, heads, width, levels, len(hops), tokens),
        grid_spec=pltpu.PrefetchScalarGridSpec(
            num_scalar_prefetch=3,
            grid=grid,
            in_specs=[wide, wide, paired] + [wide] * late + [wide, paired] + [whole] * (len(hops) + 2),
            out_specs=[wide] * late + [narrow, wide],
        ),
        out_shape=[full] * late
        + [
            jax.ShapeDtypeStruct((row_count, grid[0] * 128), F32),
            jax.ShapeDtypeStruct((row_count, columns), F32),
        ],
        compiler_params=params(),
        cost_estimate=pl.CostEstimate(flops=1, bytes_accessed=1, transcendentals=1),
        name="scores",
    )(
        where,
        key_len,
        linear_scale,
        query_rows,
        key_rows,
        both_keys,
        *[far_keys[level] for level in range(1, levels)],
        value_rows,
        both_values,
        *hops,
        near,
        far,
    )
    return pl.pallas_call(
        functools.partial(finish_kernel, late, width),
        grid=grid,
        in_specs=[narrow, wide] + [wide] * (2 * late),
        out_specs=wide,
        out_shape=full,
        compiler_params=params(),
        name="finish",
    )(factors, base, *weights, *[far_values[level] for level in range(1, levels)])


def solution(mesh):
    return jax.shard_map(
        shards,
        mesh=mesh,
        in_specs=(
            P(("groups", "seq"), "head"),
            P(("groups", "seq"), "head"),
            P(("groups", "seq"), "head"),
            P("groups"),
            P("head"),
        ),
        out_specs=P(("groups", "seq"), "head"),
        check_vma=False,
    )
```

```python
import functools
import math

import jax
import jax.numpy as jnp
from jax import lax
from jax.experimental import pallas as pl
from jax.experimental.pallas import tpu as pltpu
from jax.sharding import PartitionSpec as P

CENTER = 1.125
TERMS = 3
HEADS_A_STEP = 4
VMEM_BYTES = 40 * 1024 * 1024
F32 = jnp.float32
BF16 = jnp.bfloat16


def feature(x):
    return jnp.where(x > 0.0, x + 1.0, jnp.exp(jnp.minimum(x, 0.0)))


def halves(x):
    high = x.astype(BF16)
    return high, (x - high.astype(F32)).astype(BF16)


def padded(count):
    return -(-count // 16) * 16


def store_packed(ref, main, sums):
    rows, extra = main.shape[0], sums.shape[0]
    ref[0:rows, :] = main.astype(BF16)
    for term in range(TERMS):
        part = sums.astype(BF16)
        sums = sums - part.astype(F32)
        ref[rows + term * extra : rows + (term + 1) * extra, :] = part


def packed_sums(ref, rows, extra):
    total = ref[rows : rows + extra, :].astype(F32)
    for term in range(1, TERMS):
        total = total + ref[rows + term * extra : rows + (term + 1) * extra, :].astype(F32)
    return total


def block_sums_kernel(heads, width, where, lengths, k_ref, v_ref, send_ref, keep_ref):
    half_heads = heads // 2
    me = where[0]
    side = lax.rem(me, 2)
    length = lengths[me]
    rows = half_heads * width
    extra = padded(half_heads)
    live = lax.broadcasted_iota(jnp.int32, (k_ref.shape[0], width), 0) < length

    def one_half(first, store):
        sums = []
        for i in range(half_heads):
            columns = pl.ds(pl.multiple_of((first + i) * width, width), width)
            mapped = jnp.where(live, feature(k_ref[:, columns].astype(F32)) - CENTER, 0.0)
            values = jnp.where(live, v_ref[:, columns].astype(F32), 0.0)
            sums.append(jnp.sum(values, axis=0, keepdims=True))
            high, low = halves(mapped)
            values = values.astype(BF16)
            store(
                i,
                lax.dot_general(
                    jnp.concatenate([high, low], axis=0),
                    jnp.concatenate([values, values], axis=0),
                    (((0,), (0,)), ((), ())),
                    preferred_element_type=F32,
                ),
            )
        sums += [jnp.zeros((1, width), F32)] * (extra - half_heads)
        return jnp.concatenate(sums, axis=0)

    def store_send(i, value):
        send_ref[i * width : (i + 1) * width, :] = value.astype(BF16)

    def store_keep(i, value):
        keep_ref[i * width : (i + 1) * width, :] = value

    sums = one_half((1 - side) * half_heads, store_send)
    for term in range(TERMS):
        part = sums.astype(BF16)
        sums = sums - part.astype(F32)
        send_ref[rows + term * extra : rows + (term + 1) * extra, :] = part
    keep_ref[rows : rows + extra, :] = one_half(side * half_heads, store_keep)


def add_packed_kernel(rows, extra, count, where, keep_ref, *refs):
    flag = where[0].astype(F32)
    main = keep_ref[0:rows, :] * flag
    sums = keep_ref[rows : rows + extra, :] * flag
    for ref in refs[:count]:
        main = main + ref[0:rows, :].astype(F32)
        sums = sums + packed_sums(ref, rows, extra)
    store_packed(refs[count], main, sums)


def partners(me, levels):
    if levels != 3:
        return [me] + [jnp.bitwise_xor(me, 1 << level) for level in range(levels)]
    pair = me // 2
    inner = lax.rem(pair + pair // 2, 2)
    return [me, jnp.bitwise_xor(me, 1), jnp.bitwise_xor(me, 4 - 2 * inner), jnp.bitwise_xor(me, 2 + 2 * inner)]


def exchanges(levels):
    count = 1 << levels
    if levels != 3:
        return [[(i, i ^ 1 << level) for i in range(count)] for level in range(1, levels)]
    cycle = [(0, 1), (1, 3), (3, 2), (2, 0)]
    return [
        [(2 * a + y, 2 * b + y) for a, b in cycle for y in (0, 1)],
        [(2 * b + y, 2 * a + y) for a, b in cycle for y in (0, 1)],
    ]


def scores_kernel(width, levels, where, lengths, q_ref, *refs):
    key_refs, refs = refs[: levels + 1], refs[levels + 1 :]
    value_refs, refs = refs[:2], refs[2:]
    weight_refs, (factor_ref, base_ref) = refs[: levels - 1], refs[levels - 1 :]
    row_count = q_ref.shape[0]
    a_step = q_ref.shape[1] // width
    column = lax.broadcasted_iota(jnp.int32, (row_count, row_count), 1)
    row = lax.broadcasted_iota(jnp.int32, (row_count, row_count), 0)
    allowed = [column < lengths[partner] for partner in partners(where[0], levels)]
    allowed[0] = allowed[0] & (column <= row)
    lane = lax.broadcasted_iota(jnp.int32, (row_count, 128), 1)
    factors = jnp.zeros((row_count, 128), F32)
    for h in range(a_step):
        at = slice(h * width, (h + 1) * width)
        queries = q_ref[:, at]
        peaks, totals, weights = [], [], []
        for which in range(levels + 1):
            s = lax.dot_general(
                queries, key_refs[which][:, at], (((1,), (1,)), ((), ())), preferred_element_type=F32
            ) * (1.0 / math.sqrt(width))
            s = jnp.where(allowed[which], s, -jnp.inf)
            peak = jnp.max(s, axis=1, keepdims=True)
            p = jnp.exp(s - peak).astype(BF16)
            peaks.append(peak)
            weights.append(p)
            totals.append(jnp.sum(p.astype(F32), axis=1, keepdims=True))
        peak = functools.reduce(jnp.maximum, peaks)
        shares = [jnp.exp(one - peak) for one in peaks]
        whole = functools.reduce(jnp.add, [a * b for a, b in zip(shares, totals)])
        shares = [share / whole for share in shares]
        base = shares[0] * jnp.dot(weights[0], value_refs[0][:, at], preferred_element_type=F32)
        base_ref[:, at] = base + shares[1] * jnp.dot(weights[1], value_refs[1][:, at], preferred_element_type=F32)
        for which in range(2, levels + 1):
            weight_refs[which - 2][:, at] = weights[which]
            factors = jnp.where(lane == (which - 2) * a_step + h, shares[which], factors)
    factor_ref[...] = factors


def linear_kernel(heads, width, hops, tokens, where, scale, q_ref, *refs):
    hop_refs, (near_ref, far_ref, out_ref) = refs[:hops], refs[hops:]
    side = lax.rem(where[0], 2)
    half_heads = heads // 2
    rows, extra = half_heads * width, padded(half_heads)
    a_step = q_ref.shape[1] // width
    first = pl.program_id(0) * a_step
    mine = (first // half_heads == side).astype(F32)
    upper = mine * side.astype(F32)
    in_half = lax.rem(first, half_heads)
    sums = (1.0 - mine) * packed_sums(far_ref, rows, extra) + upper * packed_sums(near_ref, rows, extra)
    for ref in hop_refs:
        sums = sums + mine * packed_sums(ref, rows, extra)
    sum_row = lax.broadcasted_iota(jnp.int32, sums.shape, 0)
    for h in range(a_step):
        at = slice(h * width, (h + 1) * width)
        block = pl.ds(pl.multiple_of((in_half + h) * width, width), width)
        prefix = (1.0 - mine) * far_ref[block, :].astype(F32) + upper * near_ref[block, :].astype(F32)
        for ref in hop_refs:
            prefix = prefix + mine * ref[block, :].astype(F32)
        mapped = feature(q_ref[:, at].astype(F32))
        high, low = halves(mapped)
        prefix_high, prefix_low = halves(prefix)
        linear = jnp.dot(
            jnp.concatenate([high, low], axis=1),
            jnp.concatenate([prefix_high, prefix_high], axis=0),
            preferred_element_type=F32,
        ) + jnp.dot(high, prefix_low, preferred_element_type=F32)
        value_sum = jnp.sum(jnp.where(sum_row == in_half + h, sums, 0.0), axis=0, keepdims=True)
        linear = linear + jnp.sum(mapped, axis=1, keepdims=True) * (CENTER * value_sum)
        out_ref[:, at] = linear * (scale[first + h] * (1.0 / (width * math.sqrt(tokens))))


def finish_kernel(late, width, factor_ref, base_ref, linear_ref, *refs):
    out_ref = refs[2 * late]
    a_step = base_ref.shape[1] // width
    for h in range(a_step):
        at = slice(h * width, (h + 1) * width)
        total = base_ref[:, at] + linear_ref[:, at]
        for which in range(late):
            lane = which * a_step + h
            total = total + factor_ref[:, lane : lane + 1] * jnp.dot(
                refs[which][:, at], refs[late + which][:, at], preferred_element_type=F32
            )
        out_ref[:, at] = total.astype(BF16)


def params():
    return pltpu.CompilerParams(vmem_limit_bytes=VMEM_BYTES)


def shards(query_rows, key_rows, value_rows, key_len, linear_scale):
    row_count, columns = query_rows.shape
    heads = linear_scale.shape[0]
    width = columns // heads
    half_heads = heads // 2
    count = lax.axis_size("seq")
    levels = count.bit_length() - 1
    late = levels - 1
    me = lax.axis_index("seq").astype(jnp.int32)
    where = me.reshape(1)
    tokens = row_count * count
    rows, extra = half_heads * width, padded(half_heads)
    packed = jax.ShapeDtypeStruct((rows + TERMS * extra, width), BF16)
    smem = pl.BlockSpec(memory_space=pltpu.SMEM)
    vmem = pl.BlockSpec(memory_space=pltpu.VMEM)

    pairs_of_blocks = count // 2
    if pairs_of_blocks <= 4:
        steps = [[(z, z + 1)] for z in range(pairs_of_blocks - 1)]
    else:
        steps = [
            [(z, z + (1 << d)) for z in range(pairs_of_blocks - (1 << d))]
            for d in range((pairs_of_blocks - 1).bit_length())
        ]
    steps = [[(2 * a + y, 2 * b + y) for a, b in pairs for y in (0, 1)] for pairs in steps]
    swaps = [(i, i ^ 1) for i in range(count)]
    turns = exchanges(levels)

    def moved(x, pairs):
        return lax.ppermute(x, "seq", pairs)

    def after(x, *done):
        return lax.optimization_barrier((x, *done))[0]

    def fenced(run, *operands):
        shapes = jax.eval_shape(run, *operands)

        def nothing(*_):
            return jax.tree.map(lambda leaf: jnp.zeros(leaf.shape, leaf.dtype), shapes)

        return lax.cond(key_len[0] > 0, run, nothing, *operands)

    def block_sums(where, key_len, key_rows, value_rows):
        send, keep = pl.pallas_call(
            functools.partial(block_sums_kernel, heads, width),
            in_specs=[smem, smem, vmem, vmem],
            out_specs=[vmem, vmem],
            out_shape=[packed, jax.ShapeDtypeStruct((rows + extra, width), F32)],
            compiler_params=params(),
            name="block_sums",
        )(where, key_len, key_rows, value_rows)
        return keep, moved(send, swaps)

    def add_packed(flag, keep, *parts):
        return pl.pallas_call(
            functools.partial(add_packed_kernel, rows, extra, len(parts)),
            in_specs=[smem] + [vmem] * (1 + len(parts)),
            out_specs=vmem,
            out_shape=packed,
            compiler_params=params(),
            name="add_packed",
        )(flag, keep, *parts)

    one = jnp.ones((1,), jnp.int32)
    far_keys = [moved(key_rows, turns[0])]
    keep, near = fenced(block_sums, where, key_len, key_rows, value_rows)
    near_keys = moved(after(key_rows, near), swaps)
    near_values = moved(after(value_rows, near), swaps)
    hops = [moved(add_packed(one, keep, after(near, *far_keys)), steps[0])]
    far_values = [moved(after(value_rows, near), turns[0])]
    far_keys += [moved(after(key_rows, hops[0]), turn) for turn in turns[1:]]
    for pairs in steps[1:]:
        hops.append(
            fenced(
                lambda keep, *parts: moved(add_packed(one, keep, *parts), pairs), keep, near, *hops
            )
        )
    far_values += [moved(after(value_rows, hops[-1]), turn) for turn in turns[1:]]
    far = fenced(
        lambda flag, keep, *parts: moved(add_packed(flag, keep, *parts), swaps),
        1 - lax.rem(where, 2),
        keep,
        *hops,
    )

    a_step = math.gcd(HEADS_A_STEP, half_heads)
    grid = (heads // a_step,)
    wide = pl.BlockSpec((row_count, a_step * width), lambda i, *_: (0, i))
    narrow = pl.BlockSpec((row_count, 128), lambda i, *_: (0, i))
    whole = pl.BlockSpec(packed.shape, lambda i, *_: (0, 0))
    full = jax.ShapeDtypeStruct((row_count, columns), BF16)
    full_f32 = jax.ShapeDtypeStruct((row_count, columns), F32)
    *weights, factors, base = pl.pallas_call(
        functools.partial(scores_kernel, width, levels),
        grid_spec=pltpu.PrefetchScalarGridSpec(
            num_scalar_prefetch=2,
            grid=grid,
            in_specs=[wide] * (1 + levels + 1 + 2),
            out_specs=[wide] * late + [narrow, wide],
        ),
        out_shape=[full] * late + [jax.ShapeDtypeStruct((row_count, grid[0] * 128), F32), full_f32],
        compiler_params=params(),
        name="scores",
    )(where, key_len, query_rows, key_rows, near_keys, *far_keys, value_rows, near_values)
    linear = pl.pallas_call(
        functools.partial(linear_kernel, heads, width, len(hops), tokens),
        grid_spec=pltpu.PrefetchScalarGridSpec(
            num_scalar_prefetch=2,
            grid=grid,
            in_specs=[wide] + [whole] * (len(hops) + 2),
            out_specs=wide,
        ),
        out_shape=full_f32,
        compiler_params=params(),
        name="linear",
    )(where, linear_scale, query_rows, *hops, near, far)
    return pl.pallas_call(
        functools.partial(finish_kernel, late, width),
        grid=grid,
        in_specs=[narrow, wide, wide] + [wide] * (2 * late),
        out_specs=wide,
        out_shape=full,
        compiler_params=params(),
        name="finish",
    )(factors, base, linear, *weights, *far_values)


def solution(mesh):
    return jax.shard_map(
        shards,
        mesh=mesh,
        in_specs=(
            P(("groups", "seq"), "head"),
            P(("groups", "seq"), "head"),
            P(("groups", "seq"), "head"),
            P("groups"),
            P("head"),
        ),
        out_specs=P(("groups", "seq"), "head"),
        check_vma=False,
    )
```

```python
import functools
import math

import jax
import jax.numpy as jnp
from jax import lax
from jax.experimental import pallas as pl
from jax.experimental.pallas import tpu as pltpu
from jax.sharding import PartitionSpec as P

CENTER = 1.125
TERMS = 3
HEADS_A_STEP = 4
VMEM_BYTES = 40 * 1024 * 1024
F32 = jnp.float32
BF16 = jnp.bfloat16


def feature(x):
    return jnp.where(x > 0.0, x + 1.0, jnp.exp(jnp.minimum(x, 0.0)))


def halves(x):
    high = x.astype(BF16)
    return high, (x - high.astype(F32)).astype(BF16)


def padded(count):
    return -(-count // 16) * 16


def store_packed(ref, main, sums):
    rows, extra = main.shape[0], sums.shape[0]
    ref[0:rows, :] = main.astype(BF16)
    for term in range(TERMS):
        part = sums.astype(BF16)
        sums = sums - part.astype(F32)
        ref[rows + term * extra : rows + (term + 1) * extra, :] = part


def packed_sums(ref, rows, extra):
    total = ref[rows : rows + extra, :].astype(F32)
    for term in range(1, TERMS):
        total = total + ref[rows + term * extra : rows + (term + 1) * extra, :].astype(F32)
    return total


def block_sums_kernel(heads, width, where, lengths, k_ref, v_ref, send_ref, keep_ref):
    half_heads = heads // 2
    me = where[0]
    side = lax.rem(me, 2)
    length = lengths[me]
    rows = half_heads * width
    extra = padded(half_heads)
    live = lax.broadcasted_iota(jnp.int32, (k_ref.shape[0], width), 0) < length

    def one_half(first, store):
        sums = []
        for i in range(half_heads):
            columns = pl.ds(pl.multiple_of((first + i) * width, width), width)
            mapped = jnp.where(live, feature(k_ref[:, columns].astype(F32)) - CENTER, 0.0)
            values = jnp.where(live, v_ref[:, columns].astype(F32), 0.0)
            sums.append(jnp.sum(values, axis=0, keepdims=True))
            high, low = halves(mapped)
            values = values.astype(BF16)
            store(
                i,
                lax.dot_general(
                    jnp.concatenate([high, low], axis=0),
                    jnp.concatenate([values, values], axis=0),
                    (((0,), (0,)), ((), ())),
                    preferred_element_type=F32,
                ),
            )
        sums += [jnp.zeros((1, width), F32)] * (extra - half_heads)
        return jnp.concatenate(sums, axis=0)

    def store_send(i, value):
        send_ref[i * width : (i + 1) * width, :] = value.astype(BF16)

    def store_keep(i, value):
        keep_ref[i * width : (i + 1) * width, :] = value

    sums = one_half((1 - side) * half_heads, store_send)
    for term in range(TERMS):
        part = sums.astype(BF16)
        sums = sums - part.astype(F32)
        send_ref[rows + term * extra : rows + (term + 1) * extra, :] = part
    keep_ref[rows : rows + extra, :] = one_half(side * half_heads, store_keep)


def add_packed_kernel(rows, extra, count, where, keep_ref, *refs):
    flag = where[0].astype(F32)
    main = keep_ref[0:rows, :] * flag
    sums = keep_ref[rows : rows + extra, :] * flag
    for ref in refs[:count]:
        main = main + ref[0:rows, :].astype(F32)
        sums = sums + packed_sums(ref, rows, extra)
    store_packed(refs[count], main, sums)


def partners(me, levels):
    if levels != 3:
        return [me] + [jnp.bitwise_xor(me, 1 << level) for level in range(levels)]
    pair = me // 2
    inner = lax.rem(pair + pair // 2, 2)
    return [me, jnp.bitwise_xor(me, 1), jnp.bitwise_xor(me, 2 + 2 * inner), jnp.bitwise_xor(me, 4 - 2 * inner)]


def exchanges(levels):
    count = 1 << levels
    if levels != 3:
        return [[(i, i ^ 1 << level) for i in range(count)] for level in range(1, levels)]
    cycle = [(0, 2), (2, 3), (3, 1), (1, 0)]
    return [
        [(2 * a + y, 2 * b + y) for a, b in cycle for y in (0, 1)],
        [(2 * b + y, 2 * a + y) for a, b in cycle for y in (0, 1)],
    ]


def scores_kernel(width, levels, where, lengths, q_ref, *refs):
    key_refs, refs = refs[: levels + 1], refs[levels + 1 :]
    value_ref, refs = refs[0], refs[1:]
    weight_refs, (factor_ref, base_ref) = refs[:levels], refs[levels:]
    row_count = q_ref.shape[0]
    a_step = q_ref.shape[1] // width
    column = lax.broadcasted_iota(jnp.int32, (row_count, row_count), 1)
    row = lax.broadcasted_iota(jnp.int32, (row_count, row_count), 0)
    allowed = [column < lengths[partner] for partner in partners(where[0], levels)]
    allowed[0] = allowed[0] & (column <= row)
    lane = lax.broadcasted_iota(jnp.int32, (row_count, 128), 1)
    factors = jnp.zeros((row_count, 128), F32)
    for h in range(a_step):
        at = slice(h * width, (h + 1) * width)
        queries = q_ref[:, at]
        peaks, totals, weights = [], [], []
        for which in range(levels + 1):
            s = lax.dot_general(
                queries, key_refs[which][:, at], (((1,), (1,)), ((), ())), preferred_element_type=F32
            ) * (1.0 / math.sqrt(width))
            s = jnp.where(allowed[which], s, -jnp.inf)
            peak = jnp.max(s, axis=1, keepdims=True)
            p = jnp.exp(s - peak).astype(BF16)
            peaks.append(peak)
            weights.append(p)
            totals.append(jnp.sum(p.astype(F32), axis=1, keepdims=True))
        peak = functools.reduce(jnp.maximum, peaks)
        shares = [jnp.exp(one - peak) for one in peaks]
        whole = functools.reduce(jnp.add, [a * b for a, b in zip(shares, totals)])
        shares = [share / whole for share in shares]
        base_ref[:, at] = shares[0] * jnp.dot(weights[0], value_ref[:, at], preferred_element_type=F32)
        for which in range(levels):
            weight_refs[which][:, at] = weights[which + 1]
            factors = jnp.where(lane == which * a_step + h, shares[which + 1], factors)
    factor_ref[...] = factors


def linear_kernel(heads, width, hops, tokens, where, scale, q_ref, factor_ref, base_ref, weight_ref, value_ref, *refs):
    hop_refs, (near_ref, far_ref, out_ref) = refs[:hops], refs[hops:]
    side = lax.rem(where[0], 2)
    half_heads = heads // 2
    rows, extra = half_heads * width, padded(half_heads)
    a_step = q_ref.shape[1] // width
    first = pl.program_id(0) * a_step
    mine = (first // half_heads == side).astype(F32)
    upper = mine * side.astype(F32)
    in_half = lax.rem(first, half_heads)
    sums = (1.0 - mine) * packed_sums(far_ref, rows, extra) + upper * packed_sums(near_ref, rows, extra)
    for ref in hop_refs:
        sums = sums + mine * packed_sums(ref, rows, extra)
    sum_row = lax.broadcasted_iota(jnp.int32, sums.shape, 0)
    for h in range(a_step):
        at = slice(h * width, (h + 1) * width)
        block = pl.ds(pl.multiple_of((in_half + h) * width, width), width)
        prefix = (1.0 - mine) * far_ref[block, :].astype(F32) + upper * near_ref[block, :].astype(F32)
        for ref in hop_refs:
            prefix = prefix + mine * ref[block, :].astype(F32)
        mapped = feature(q_ref[:, at].astype(F32))
        high, low = halves(mapped)
        prefix_high, prefix_low = halves(prefix)
        linear = jnp.dot(
            jnp.concatenate([high, low], axis=1),
            jnp.concatenate([prefix_high, prefix_high], axis=0),
            preferred_element_type=F32,
        ) + jnp.dot(high, prefix_low, preferred_element_type=F32)
        value_sum = jnp.sum(jnp.where(sum_row == in_half + h, sums, 0.0), axis=0, keepdims=True)
        linear = linear + jnp.sum(mapped, axis=1, keepdims=True) * (CENTER * value_sum)
        near = jnp.dot(weight_ref[:, at], value_ref[:, at], preferred_element_type=F32)
        total = base_ref[:, at] + factor_ref[:, h : h + 1] * near
        out_ref[:, at] = total + linear * (scale[first + h] * (1.0 / (width * math.sqrt(tokens))))


def finish_kernel(late, width, factor_ref, base_ref, *refs):
    out_ref = refs[2 * late]
    a_step = base_ref.shape[1] // width
    for h in range(a_step):
        at = slice(h * width, (h + 1) * width)
        total = base_ref[:, at]
        for which in range(late):
            lane = (which + 1) * a_step + h
            total = total + factor_ref[:, lane : lane + 1] * jnp.dot(
                refs[which][:, at], refs[late + which][:, at], preferred_element_type=F32
            )
        out_ref[:, at] = total.astype(BF16)


def params():
    return pltpu.CompilerParams(vmem_limit_bytes=VMEM_BYTES)


def shards(query_rows, key_rows, value_rows, key_len, linear_scale):
    row_count, columns = query_rows.shape
    heads = linear_scale.shape[0]
    width = columns // heads
    half_heads = heads // 2
    count = lax.axis_size("seq")
    levels = count.bit_length() - 1
    late = levels - 1
    me = lax.axis_index("seq").astype(jnp.int32)
    where = me.reshape(1)
    tokens = row_count * count
    rows, extra = half_heads * width, padded(half_heads)
    packed = jax.ShapeDtypeStruct((rows + TERMS * extra, width), BF16)
    smem = pl.BlockSpec(memory_space=pltpu.SMEM)
    vmem = pl.BlockSpec(memory_space=pltpu.VMEM)

    pairs_of_blocks = count // 2
    if pairs_of_blocks <= 4:
        steps = [[(z, z + 1)] for z in range(pairs_of_blocks - 1)]
    else:
        steps = [
            [(z, z + (1 << d)) for z in range(pairs_of_blocks - (1 << d))]
            for d in range((pairs_of_blocks - 1).bit_length())
        ]
    steps = [[(2 * a + y, 2 * b + y) for a, b in pairs for y in (0, 1)] for pairs in steps]
    swaps = [(i, i ^ 1) for i in range(count)]
    turns = exchanges(levels)

    def moved(x, pairs):
        return lax.ppermute(x, "seq", pairs)

    def after(x, *done):
        return lax.optimization_barrier((x, *done))[0]

    def fenced(run, *operands):
        shapes = jax.eval_shape(run, *operands)

        def nothing(*_):
            return jax.tree.map(lambda leaf: jnp.zeros(leaf.shape, leaf.dtype), shapes)

        return lax.cond(key_len[0] > 0, run, nothing, *operands)

    def block_sums(where, key_len, key_rows, value_rows):
        send, keep = pl.pallas_call(
            functools.partial(block_sums_kernel, heads, width),
            in_specs=[smem, smem, vmem, vmem],
            out_specs=[vmem, vmem],
            out_shape=[packed, jax.ShapeDtypeStruct((rows + extra, width), F32)],
            compiler_params=params(),
            name="block_sums",
        )(where, key_len, key_rows, value_rows)
        return keep, moved(send, swaps)

    def add_packed(flag, keep, *parts):
        return pl.pallas_call(
            functools.partial(add_packed_kernel, rows, extra, len(parts)),
            in_specs=[smem] + [vmem] * (1 + len(parts)),
            out_specs=vmem,
            out_shape=packed,
            compiler_params=params(),
            name="add_packed",
        )(flag, keep, *parts)

    a_step = math.gcd(HEADS_A_STEP, half_heads)
    grid = (heads // a_step,)
    wide = pl.BlockSpec((row_count, a_step * width), lambda i, *_: (0, i))
    narrow = pl.BlockSpec((row_count, 128), lambda i, *_: (0, i))
    whole = pl.BlockSpec(packed.shape, lambda i, *_: (0, 0))
    full = jax.ShapeDtypeStruct((row_count, columns), BF16)
    full_f32 = jax.ShapeDtypeStruct((row_count, columns), F32)

    def scores(where, key_len, query_rows, key_rows, value_rows, *keys):
        return pl.pallas_call(
            functools.partial(scores_kernel, width, levels),
            grid_spec=pltpu.PrefetchScalarGridSpec(
                num_scalar_prefetch=2,
                grid=grid,
                in_specs=[wide] * (1 + levels + 1 + 1),
                out_specs=[wide] * levels + [narrow, wide],
            ),
            out_shape=[full] * levels + [jax.ShapeDtypeStruct((row_count, grid[0] * 128), F32), full_f32],
            compiler_params=params(),
            name="scores",
        )(where, key_len, query_rows, key_rows, *keys, value_rows)

    one = jnp.ones((1,), jnp.int32)
    far_keys = [moved(key_rows, turns[0])]
    keep, near = fenced(block_sums, where, key_len, key_rows, value_rows)
    near_keys = moved(after(key_rows, near), swaps)
    near_values = moved(after(value_rows, near), swaps)
    hops = [moved(add_packed(one, keep, after(near, *far_keys)), steps[0])]
    far_keys += [moved(after(key_rows, near), turn) for turn in turns[1:]]
    hops.append(moved(add_packed(one, keep, near, *hops), steps[1]))
    far_values = [moved(after(value_rows, *far_keys), turns[0])]
    far_values += [moved(after(value_rows, *hops), turn) for turn in turns[1:]]

    def last_hop(keep, parts, *operands):
        for pairs in steps[2:]:
            parts = [*parts, moved(add_packed(one, keep, *parts), pairs)]
        return parts[1:], scores(*operands)

    hops, (*weights, factors, base) = fenced(
        last_hop, keep, [near, *hops], where, key_len, query_rows, key_rows, value_rows, near_keys, *far_keys
    )
    far = fenced(
        lambda flag, keep, *parts: moved(add_packed(flag, keep, *parts), swaps),
        1 - lax.rem(where, 2),
        keep,
        *hops,
    )
    base = pl.pallas_call(
        functools.partial(linear_kernel, heads, width, len(hops), tokens),
        grid_spec=pltpu.PrefetchScalarGridSpec(
            num_scalar_prefetch=2,
            grid=grid,
            in_specs=[wide, narrow] + [wide] * 3 + [whole] * (len(hops) + 2),
            out_specs=wide,
        ),
        out_shape=full_f32,
        compiler_params=params(),
        name="linear",
    )(where, linear_scale, query_rows, factors, base, weights[0], near_values, *hops, near, far)
    return pl.pallas_call(
        functools.partial(finish_kernel, late, width),
        grid=grid,
        in_specs=[narrow, wide] + [wide] * (2 * late),
        out_specs=wide,
        out_shape=full,
        compiler_params=params(),
        name="finish",
    )(factors, base, *weights[1:], *far_values)


def solution(mesh):
    return jax.shard_map(
        shards,
        mesh=mesh,
        in_specs=(
            P(("groups", "seq"), "head"),
            P(("groups", "seq"), "head"),
            P(("groups", "seq"), "head"),
            P("groups"),
            P("head"),
        ),
        out_specs=P(("groups", "seq"), "head"),
        check_vma=False,
    )
```

```python
import functools
import math

import jax
import jax.numpy as jnp
from jax import lax
from jax.experimental import pallas as pl
from jax.experimental.pallas import tpu as pltpu
from jax.sharding import PartitionSpec as P

CENTER = 1.125
TERMS = 3
HEADS_A_STEP = 4
VMEM_BYTES = 40 * 1024 * 1024
F32 = jnp.float32
BF16 = jnp.bfloat16


def feature(x):
    return jnp.where(x > 0.0, x + 1.0, jnp.exp(jnp.minimum(x, 0.0)))


def halves(x):
    high = x.astype(BF16)
    return high, (x - high.astype(F32)).astype(BF16)


def padded(count):
    return -(-count // 16) * 16


def store_packed(ref, main, sums):
    rows, extra = main.shape[0], sums.shape[0]
    ref[0:rows, :] = main.astype(BF16)
    for term in range(TERMS):
        part = sums.astype(BF16)
        sums = sums - part.astype(F32)
        ref[rows + term * extra : rows + (term + 1) * extra, :] = part


def packed_sums(ref, rows, extra):
    total = ref[rows : rows + extra, :].astype(F32)
    for term in range(1, TERMS):
        total = total + ref[rows + term * extra : rows + (term + 1) * extra, :].astype(F32)
    return total


def block_sums_kernel(heads, width, where, lengths, k_ref, v_ref, send_ref, keep_ref):
    half_heads = heads // 2
    me = where[0]
    side = lax.rem(me, 2)
    length = lengths[me]
    rows = half_heads * width
    extra = padded(half_heads)
    live = lax.broadcasted_iota(jnp.int32, (k_ref.shape[0], width), 0) < length

    def one_half(first, store):
        sums = []
        for i in range(half_heads):
            columns = pl.ds(pl.multiple_of((first + i) * width, width), width)
            mapped = jnp.where(live, feature(k_ref[:, columns].astype(F32)) - CENTER, 0.0)
            values = jnp.where(live, v_ref[:, columns].astype(F32), 0.0)
            sums.append(jnp.sum(values, axis=0, keepdims=True))
            high, low = halves(mapped)
            values = values.astype(BF16)
            store(
                i,
                lax.dot_general(
                    jnp.concatenate([high, low], axis=0),
                    jnp.concatenate([values, values], axis=0),
                    (((0,), (0,)), ((), ())),
                    preferred_element_type=F32,
                ),
            )
        sums += [jnp.zeros((1, width), F32)] * (extra - half_heads)
        return jnp.concatenate(sums, axis=0)

    def store_send(i, value):
        send_ref[i * width : (i + 1) * width, :] = value.astype(BF16)

    def store_keep(i, value):
        keep_ref[i * width : (i + 1) * width, :] = value

    sums = one_half((1 - side) * half_heads, store_send)
    for term in range(TERMS):
        part = sums.astype(BF16)
        sums = sums - part.astype(F32)
        send_ref[rows + term * extra : rows + (term + 1) * extra, :] = part
    keep_ref[rows : rows + extra, :] = one_half(side * half_heads, store_keep)


def add_packed_kernel(rows, extra, count, where, keep_ref, *refs):
    flag = where[0].astype(F32)
    main = keep_ref[0:rows, :] * flag
    sums = keep_ref[rows : rows + extra, :] * flag
    for ref in refs[:count]:
        main = main + ref[0:rows, :].astype(F32)
        sums = sums + packed_sums(ref, rows, extra)
    store_packed(refs[count], main, sums)


def partners(me, levels):
    if levels != 3:
        return [me] + [jnp.bitwise_xor(me, 1 << level) for level in range(levels)]
    pair = me // 2
    inner = lax.rem(pair + pair // 2, 2)
    return [me, jnp.bitwise_xor(me, 1), jnp.bitwise_xor(me, 2 + 2 * inner), jnp.bitwise_xor(me, 4 - 2 * inner)]


def exchanges(levels):
    count = 1 << levels
    if levels != 3:
        return [[(i, i ^ 1 << level) for i in range(count)] for level in range(1, levels)]
    cycle = [(0, 2), (2, 3), (3, 1), (1, 0)]
    return [
        [(2 * a + y, 2 * b + y) for a, b in cycle for y in (0, 1)],
        [(2 * b + y, 2 * a + y) for a, b in cycle for y in (0, 1)],
    ]


def scores_kernel(width, levels, where, lengths, q_ref, *refs):
    key_refs, refs = refs[: levels + 1], refs[levels + 1 :]
    value_ref, refs = refs[0], refs[1:]
    weight_refs, (factor_ref, base_ref) = refs[:levels], refs[levels:]
    row_count = q_ref.shape[0]
    a_step = q_ref.shape[1] // width
    column = lax.broadcasted_iota(jnp.int32, (row_count, row_count), 1)
    row = lax.broadcasted_iota(jnp.int32, (row_count, row_count), 0)
    allowed = [column < lengths[partner] for partner in partners(where[0], levels)]
    allowed[0] = allowed[0] & (column <= row)
    lane = lax.broadcasted_iota(jnp.int32, (row_count, 128), 1)
    factors = jnp.zeros((row_count, 128), F32)
    for h in range(a_step):
        at = slice(h * width, (h + 1) * width)
        queries = q_ref[:, at]
        peaks, totals, weights = [], [], []
        for which in range(levels + 1):
            s = lax.dot_general(
                queries, key_refs[which][:, at], (((1,), (1,)), ((), ())), preferred_element_type=F32
            ) * (1.0 / math.sqrt(width))
            s = jnp.where(allowed[which], s, -jnp.inf)
            peak = jnp.max(s, axis=1, keepdims=True)
            p = jnp.exp(s - peak).astype(BF16)
            peaks.append(peak)
            weights.append(p)
            totals.append(jnp.sum(p.astype(F32), axis=1, keepdims=True))
        peak = functools.reduce(jnp.maximum, peaks)
        shares = [jnp.exp(one - peak) for one in peaks]
        whole = functools.reduce(jnp.add, [a * b for a, b in zip(shares, totals)])
        shares = [share / whole for share in shares]
        base_ref[:, at] = shares[0] * jnp.dot(weights[0], value_ref[:, at], preferred_element_type=F32)
        for which in range(levels):
            weight_refs[which][:, at] = weights[which + 1]
            factors = jnp.where(lane == which * a_step + h, shares[which + 1], factors)
    factor_ref[...] = factors


def linear_kernel(heads, width, own, parts, tokens, where, scale, q_ref, factor_ref, base_ref, weight_ref, value_ref, *refs):
    part_refs, out_ref = refs[:parts], refs[parts]
    side = lax.rem(where[0], 2)
    half_heads = heads // 2
    rows, extra = half_heads * width, padded(half_heads)
    a_step = q_ref.shape[1] // width
    in_half = pl.program_id(0) * a_step
    first = (side if own else 1 - side) * half_heads + in_half
    flags = [1.0] * (parts - 1) + [side.astype(F32) if own else 1.0]
    sums = functools.reduce(
        jnp.add, [flag * packed_sums(ref, rows, extra) for flag, ref in zip(flags, part_refs)]
    )
    sum_row = lax.broadcasted_iota(jnp.int32, sums.shape, 0)
    for h in range(a_step):
        at = slice(h * width, (h + 1) * width)
        block = pl.ds(pl.multiple_of((in_half + h) * width, width), width)
        mapped = feature(q_ref[:, at].astype(F32))
        high, low = halves(mapped)
        if own:
            prefix = functools.reduce(
                jnp.add, [flag * ref[block, :].astype(F32) for flag, ref in zip(flags, part_refs)]
            )
            prefix, rest = halves(prefix)
        else:
            prefix = part_refs[0][block, :]
        linear = jnp.dot(
            jnp.concatenate([high, low], axis=1),
            jnp.concatenate([prefix, prefix], axis=0),
            preferred_element_type=F32,
        )
        if own:
            linear = linear + jnp.dot(high, rest, preferred_element_type=F32)
        value_sum = jnp.sum(jnp.where(sum_row == in_half + h, sums, 0.0), axis=0, keepdims=True)
        linear = linear + jnp.sum(mapped, axis=1, keepdims=True) * (CENTER * value_sum)
        near = jnp.dot(weight_ref[:, at], value_ref[:, at], preferred_element_type=F32)
        total = base_ref[:, at] + factor_ref[:, h : h + 1] * near
        out_ref[:, at] = total + linear * (scale[first + h] * (1.0 / (width * math.sqrt(tokens))))


def finish_kernel(late, width, where, factor_ref, own_ref, other_ref, *refs):
    out_ref = refs[2 * late]
    a_step = own_ref.shape[1] // width
    own = pl.program_id(0) // (pl.num_programs(0) // 2) == lax.rem(where[0], 2)
    for h in range(a_step):
        at = slice(h * width, (h + 1) * width)
        total = jnp.where(own, own_ref[:, at], other_ref[:, at])
        for which in range(late):
            lane = (which + 1) * a_step + h
            total = total + factor_ref[:, lane : lane + 1] * jnp.dot(
                refs[which][:, at], refs[late + which][:, at], preferred_element_type=F32
            )
        out_ref[:, at] = total.astype(BF16)


def params():
    return pltpu.CompilerParams(vmem_limit_bytes=VMEM_BYTES)


def shards(query_rows, key_rows, value_rows, key_len, linear_scale):
    row_count, columns = query_rows.shape
    heads = linear_scale.shape[0]
    width = columns // heads
    half_heads = heads // 2
    count = lax.axis_size("seq")
    levels = count.bit_length() - 1
    late = levels - 1
    me = lax.axis_index("seq").astype(jnp.int32)
    where = me.reshape(1)
    tokens = row_count * count
    rows, extra = half_heads * width, padded(half_heads)
    packed = jax.ShapeDtypeStruct((rows + TERMS * extra, width), BF16)
    smem = pl.BlockSpec(memory_space=pltpu.SMEM)
    vmem = pl.BlockSpec(memory_space=pltpu.VMEM)

    pairs_of_blocks = count // 2
    if pairs_of_blocks <= 4:
        steps = [[(z, z + 1)] for z in range(pairs_of_blocks - 1)]
    else:
        steps = [
            [(z, z + (1 << d)) for z in range(pairs_of_blocks - (1 << d))]
            for d in range((pairs_of_blocks - 1).bit_length())
        ]
    steps = [[(2 * a + y, 2 * b + y) for a, b in pairs for y in (0, 1)] for pairs in steps]
    swaps = [(i, i ^ 1) for i in range(count)]
    turns = exchanges(levels)

    def moved(x, pairs):
        return lax.ppermute(x, "seq", pairs)

    def after(x, *done):
        return lax.optimization_barrier((x, *done))[0]

    def fenced(run, *operands):
        shapes = jax.eval_shape(run, *operands)

        def nothing(*_):
            return jax.tree.map(lambda leaf: jnp.zeros(leaf.shape, leaf.dtype), shapes)

        return lax.cond(key_len[0] > 0, run, nothing, *operands)

    def block_sums(where, key_len, key_rows, value_rows):
        send, keep = pl.pallas_call(
            functools.partial(block_sums_kernel, heads, width),
            in_specs=[smem, smem, vmem, vmem],
            out_specs=[vmem, vmem],
            out_shape=[packed, jax.ShapeDtypeStruct((rows + extra, width), F32)],
            compiler_params=params(),
            name="block_sums",
        )(where, key_len, key_rows, value_rows)
        return keep, moved(send, swaps)

    def add_packed(flag, keep, *parts):
        return pl.pallas_call(
            functools.partial(add_packed_kernel, rows, extra, len(parts)),
            in_specs=[smem] + [vmem] * (1 + len(parts)),
            out_specs=vmem,
            out_shape=packed,
            compiler_params=params(),
            name="add_packed",
        )(flag, keep, *parts)

    a_step = math.gcd(HEADS_A_STEP, half_heads)
    grid = (heads // a_step,)
    wide = pl.BlockSpec((row_count, a_step * width), lambda i, *_: (0, i))
    narrow = pl.BlockSpec((row_count, 128), lambda i, *_: (0, i))
    whole = pl.BlockSpec(packed.shape, lambda i, *_: (0, 0))
    full = jax.ShapeDtypeStruct((row_count, columns), BF16)
    full_f32 = jax.ShapeDtypeStruct((row_count, columns), F32)

    def scores(where, key_len, query_rows, key_rows, value_rows, *keys):
        return pl.pallas_call(
            functools.partial(scores_kernel, width, levels),
            grid_spec=pltpu.PrefetchScalarGridSpec(
                num_scalar_prefetch=2,
                grid=grid,
                in_specs=[wide] * (1 + levels + 1 + 1),
                out_specs=[wide] * levels + [narrow, wide],
            ),
            out_shape=[full] * levels + [jax.ShapeDtypeStruct((row_count, grid[0] * 128), F32), full_f32],
            compiler_params=params(),
            name="scores",
        )(where, key_len, query_rows, key_rows, *keys, value_rows)

    one = jnp.ones((1,), jnp.int32)
    far_keys = [moved(key_rows, turns[0])]
    keep, near = fenced(block_sums, where, key_len, key_rows, value_rows)
    near_keys = moved(after(key_rows, near), swaps)
    near_values = moved(after(value_rows, near), swaps)
    hops = [moved(add_packed(one, keep, near), steps[0])]
    far_keys += [moved(after(key_rows, near), turn) for turn in turns[1:]]
    hops.append(moved(add_packed(one, keep, after(near, far_keys[0]), *hops), steps[1]))
    far_values = [moved(after(value_rows, near_keys, *far_keys), turns[0])]

    def last_hop(keep, parts, *operands):
        for pairs in steps[2:]:
            parts = [*parts, moved(add_packed(one, keep, *parts), pairs)]
        return parts[1:], scores(*operands)

    hops, (*weights, factors, base) = fenced(
        last_hop, keep, [near, *hops], where, key_len, query_rows, key_rows, value_rows, near_keys, *far_keys
    )
    far_values += [moved(after(value_rows, *hops), turn) for turn in turns[1:]]

    half_grid = grid[0] // 2
    half_f32 = jax.ShapeDtypeStruct((row_count, columns // 2), F32)

    def linear(own, where, linear_scale, query_rows, factors, base, weights, near_values, *parts):
        def at(i, where, scale):
            side = lax.rem(where[0], 2)
            return 0, (side if own else 1 - side) * half_grid + i

        chosen = pl.BlockSpec((row_count, a_step * width), at)
        return pl.pallas_call(
            functools.partial(linear_kernel, heads, width, own, len(parts), tokens),
            grid_spec=pltpu.PrefetchScalarGridSpec(
                num_scalar_prefetch=2,
                grid=(half_grid,),
                in_specs=[chosen, pl.BlockSpec((row_count, 128), at)] + [chosen] * 3 + [whole] * len(parts),
                out_specs=wide,
            ),
            out_shape=half_f32,
            compiler_params=params(),
            name="linear_own" if own else "linear_other",
        )(where, linear_scale, query_rows, factors, base, weights, near_values, *parts)

    operands = (where, linear_scale, query_rows, factors, base, weights[0], near_values)

    def last_exchange(flag, keep, near, hops, *operands):
        return moved(add_packed(flag, keep, *hops), swaps), linear(True, *operands, *hops, near)

    far, own = fenced(last_exchange, 1 - lax.rem(where, 2), keep, near, hops, *operands)
    other = linear(False, *operands, far)
    half = pl.BlockSpec((row_count, a_step * width), lambda i, *_: (0, lax.rem(i, half_grid)))
    return pl.pallas_call(
        functools.partial(finish_kernel, late, width),
        grid_spec=pltpu.PrefetchScalarGridSpec(
            num_scalar_prefetch=1,
            grid=grid,
            in_specs=[narrow, half, half] + [wide] * (2 * late),
            out_specs=wide,
        ),
        out_shape=full,
        compiler_params=params(),
        name="finish",
    )(where, factors, own, other, *weights[1:], *far_values)


def solution(mesh):
    return jax.shard_map(
        shards,
        mesh=mesh,
        in_specs=(
            P(("groups", "seq"), "head"),
            P(("groups", "seq"), "head"),
            P(("groups", "seq"), "head"),
            P("groups"),
            P("head"),
        ),
        out_specs=P(("groups", "seq"), "head"),
        check_vma=False,
    )
```

```python
import functools
import math

import jax
import jax.numpy as jnp
from jax import lax
from jax.experimental import pallas as pl
from jax.experimental.pallas import tpu as pltpu
from jax.sharding import PartitionSpec as P

CENTER = 1.125
TERMS = 3
HEADS_A_STEP = 4
VMEM_BYTES = 40 * 1024 * 1024
F32 = jnp.float32
BF16 = jnp.bfloat16


def feature(x):
    return jnp.where(x > 0.0, x + 1.0, jnp.exp(jnp.minimum(x, 0.0)))


def halves(x):
    high = x.astype(BF16)
    return high, (x - high.astype(F32)).astype(BF16)


def padded(count):
    return -(-count // 16) * 16


def store_packed(ref, main, sums):
    rows, extra = main.shape[0], sums.shape[0]
    ref[0:rows, :] = main.astype(BF16)
    for term in range(TERMS):
        part = sums.astype(BF16)
        sums = sums - part.astype(F32)
        ref[rows + term * extra : rows + (term + 1) * extra, :] = part


def packed_sums(ref, rows, extra):
    total = ref[rows : rows + extra, :].astype(F32)
    for term in range(1, TERMS):
        total = total + ref[rows + term * extra : rows + (term + 1) * extra, :].astype(F32)
    return total


def block_sums_kernel(heads, width, where, lengths, k_ref, v_ref, send_ref, keep_ref):
    half_heads = heads // 2
    me = where[0]
    side = lax.rem(me, 2)
    length = lengths[me]
    rows = half_heads * width
    extra = padded(half_heads)
    live = lax.broadcasted_iota(jnp.int32, (k_ref.shape[0], width), 0) < length

    def one_half(first, store):
        sums = []
        for i in range(half_heads):
            columns = pl.ds(pl.multiple_of((first + i) * width, width), width)
            mapped = jnp.where(live, feature(k_ref[:, columns].astype(F32)) - CENTER, 0.0)
            values = jnp.where(live, v_ref[:, columns].astype(F32), 0.0)
            sums.append(jnp.sum(values, axis=0, keepdims=True))
            high, low = halves(mapped)
            values = values.astype(BF16)
            store(
                i,
                lax.dot_general(
                    jnp.concatenate([high, low], axis=0),
                    jnp.concatenate([values, values], axis=0),
                    (((0,), (0,)), ((), ())),
                    preferred_element_type=F32,
                ),
            )
        sums += [jnp.zeros((1, width), F32)] * (extra - half_heads)
        return jnp.concatenate(sums, axis=0)

    def store_send(i, value):
        send_ref[i * width : (i + 1) * width, :] = value.astype(BF16)

    def store_keep(i, value):
        keep_ref[i * width : (i + 1) * width, :] = value

    sums = one_half((1 - side) * half_heads, store_send)
    for term in range(TERMS):
        part = sums.astype(BF16)
        sums = sums - part.astype(F32)
        send_ref[rows + term * extra : rows + (term + 1) * extra, :] = part
    keep_ref[rows : rows + extra, :] = one_half(side * half_heads, store_keep)


def add_packed_kernel(rows, extra, count, where, keep_ref, *refs):
    flag = where[0].astype(F32)
    main = keep_ref[0:rows, :] * flag
    sums = keep_ref[rows : rows + extra, :] * flag
    for ref in refs[:count]:
        main = main + ref[0:rows, :].astype(F32)
        sums = sums + packed_sums(ref, rows, extra)
    store_packed(refs[count], main, sums)


def partners(me, levels):
    if levels != 3:
        return [me] + [jnp.bitwise_xor(me, 1 << level) for level in range(levels)]
    pair = me // 2
    inner = lax.rem(pair + pair // 2, 2)
    return [me, jnp.bitwise_xor(me, 1), jnp.bitwise_xor(me, 2 + 2 * inner), jnp.bitwise_xor(me, 4 - 2 * inner)]


def exchanges(levels):
    count = 1 << levels
    if levels != 3:
        return [[(i, i ^ 1 << level) for i in range(count)] for level in range(1, levels)]
    cycle = [(0, 2), (2, 3), (3, 1), (1, 0)]
    return [
        [(2 * a + y, 2 * b + y) for a, b in cycle for y in (0, 1)],
        [(2 * b + y, 2 * a + y) for a, b in cycle for y in (0, 1)],
    ]


def scores_kernel(width, levels, where, lengths, q_ref, *refs):
    key_refs, refs = refs[: levels + 1], refs[levels + 1 :]
    value_ref, refs = refs[0], refs[1:]
    weight_refs, (factor_ref, base_ref) = refs[:levels], refs[levels:]
    row_count = q_ref.shape[0]
    a_step = q_ref.shape[1] // width
    column = lax.broadcasted_iota(jnp.int32, (row_count, row_count), 1)
    row = lax.broadcasted_iota(jnp.int32, (row_count, row_count), 0)
    allowed = [column < lengths[partner] for partner in partners(where[0], levels)]
    allowed[0] = allowed[0] & (column <= row)
    lane = lax.broadcasted_iota(jnp.int32, (row_count, 128), 1)
    factors = jnp.zeros((row_count, 128), F32)
    for h in range(a_step):
        at = slice(h * width, (h + 1) * width)
        queries = q_ref[:, at]
        peaks, totals, weights = [], [], []
        for which in range(levels + 1):
            s = lax.dot_general(
                queries, key_refs[which][:, at], (((1,), (1,)), ((), ())), preferred_element_type=F32
            ) * (1.0 / math.sqrt(width))
            s = jnp.where(allowed[which], s, -jnp.inf)
            peak = jnp.max(s, axis=1, keepdims=True)
            p = jnp.exp(s - peak).astype(BF16)
            peaks.append(peak)
            weights.append(p)
            totals.append(jnp.sum(p.astype(F32), axis=1, keepdims=True))
        peak = functools.reduce(jnp.maximum, peaks)
        shares = [jnp.exp(one - peak) for one in peaks]
        whole = functools.reduce(jnp.add, [a * b for a, b in zip(shares, totals)])
        shares = [share / whole for share in shares]
        base_ref[:, at] = shares[0] * jnp.dot(weights[0], value_ref[:, at], preferred_element_type=F32)
        for which in range(levels):
            weight_refs[which][:, at] = weights[which + 1]
            factors = jnp.where(lane == which * a_step + h, shares[which + 1], factors)
    factor_ref[...] = factors


def linear_kernel(heads, width, own, parts, tokens, where, scale, q_ref, factor_ref, base_ref, weight_ref, value_ref, *refs):
    part_refs, out_ref = refs[:parts], refs[parts]
    side = lax.rem(where[0], 2)
    half_heads = heads // 2
    rows, extra = half_heads * width, padded(half_heads)
    a_step = q_ref.shape[1] // width
    in_half = pl.program_id(0) * a_step
    first = (side if own else 1 - side) * half_heads + in_half
    flags = [1.0] * (parts - 1) + [side.astype(F32) if own else 1.0]
    sums = functools.reduce(
        jnp.add, [flag * packed_sums(ref, rows, extra) for flag, ref in zip(flags, part_refs)]
    )
    sum_row = lax.broadcasted_iota(jnp.int32, sums.shape, 0)
    for h in range(a_step):
        at = slice(h * width, (h + 1) * width)
        block = pl.ds(pl.multiple_of((in_half + h) * width, width), width)
        mapped = feature(q_ref[:, at].astype(F32))
        high, low = halves(mapped)
        if own:
            prefix = functools.reduce(
                jnp.add, [flag * ref[block, :].astype(F32) for flag, ref in zip(flags, part_refs)]
            )
            prefix, rest = halves(prefix)
        else:
            prefix = part_refs[0][block, :]
        linear = jnp.dot(
            jnp.concatenate([high, low], axis=1),
            jnp.concatenate([prefix, prefix], axis=0),
            preferred_element_type=F32,
        )
        if own:
            linear = linear + jnp.dot(high, rest, preferred_element_type=F32)
        value_sum = jnp.sum(jnp.where(sum_row == in_half + h, sums, 0.0), axis=0, keepdims=True)
        linear = linear + jnp.sum(mapped, axis=1, keepdims=True) * (CENTER * value_sum)
        near = jnp.dot(weight_ref[:, at], value_ref[:, at], preferred_element_type=F32)
        total = base_ref[:, at] + factor_ref[:, h : h + 1] * near
        out_ref[:, at] = total + linear * (scale[first + h] * (1.0 / (width * math.sqrt(tokens))))


def finish_kernel(late, width, where, factor_ref, own_ref, other_ref, *refs):
    weight_refs, first_refs, value_refs = refs[:late], refs[late:-late], refs[-late:-1]
    out_ref = refs[-1]
    a_step = own_ref.shape[1] // width
    own = pl.program_id(0) // (pl.num_programs(0) // 2) == lax.rem(where[0], 2)
    for h in range(a_step):
        at = slice(h * width, (h + 1) * width)
        total = jnp.where(own, own_ref[:, at], other_ref[:, at])
        values = [functools.reduce(jnp.add, [ref[:, at] for ref in first_refs])]
        values += [ref[:, at] for ref in value_refs]
        for which in range(late):
            lane = (which + 1) * a_step + h
            total = total + factor_ref[:, lane : lane + 1] * jnp.dot(
                weight_refs[which][:, at], values[which], preferred_element_type=F32
            )
        out_ref[:, at] = total.astype(BF16)


def params():
    return pltpu.CompilerParams(vmem_limit_bytes=VMEM_BYTES)


def shards(query_rows, key_rows, value_rows, key_len, linear_scale):
    row_count, columns = query_rows.shape
    heads = linear_scale.shape[0]
    width = columns // heads
    half_heads = heads // 2
    count = lax.axis_size("seq")
    levels = count.bit_length() - 1
    late = levels - 1
    me = lax.axis_index("seq").astype(jnp.int32)
    where = me.reshape(1)
    tokens = row_count * count
    rows, extra = half_heads * width, padded(half_heads)
    packed = jax.ShapeDtypeStruct((rows + TERMS * extra, width), BF16)
    smem = pl.BlockSpec(memory_space=pltpu.SMEM)
    vmem = pl.BlockSpec(memory_space=pltpu.VMEM)

    pairs_of_blocks = count // 2
    if pairs_of_blocks <= 4:
        steps = [[(z, z + 1)] for z in range(pairs_of_blocks - 1)]
    else:
        steps = [
            [(z, z + (1 << d)) for z in range(pairs_of_blocks - (1 << d))]
            for d in range((pairs_of_blocks - 1).bit_length())
        ]
    steps = [[(2 * a + y, 2 * b + y) for a, b in pairs for y in (0, 1)] for pairs in steps]
    swaps = [(i, i ^ 1) for i in range(count)]
    turns = exchanges(levels)

    def moved(x, pairs):
        return lax.ppermute(x, "seq", pairs)

    def after(x, *done):
        return lax.optimization_barrier((x, *done))[0]

    def fenced(run, *operands):
        shapes = jax.eval_shape(run, *operands)

        def nothing(*_):
            return jax.tree.map(lambda leaf: jnp.zeros(leaf.shape, leaf.dtype), shapes)

        return lax.cond(key_len[0] > 0, run, nothing, *operands)

    def block_sums(where, key_len, key_rows, value_rows):
        send, keep = pl.pallas_call(
            functools.partial(block_sums_kernel, heads, width),
            in_specs=[smem, smem, vmem, vmem],
            out_specs=[vmem, vmem],
            out_shape=[packed, jax.ShapeDtypeStruct((rows + extra, width), F32)],
            compiler_params=params(),
            name="block_sums",
        )(where, key_len, key_rows, value_rows)
        return keep, moved(send, swaps)

    def add_packed(flag, keep, *parts):
        return pl.pallas_call(
            functools.partial(add_packed_kernel, rows, extra, len(parts)),
            in_specs=[smem] + [vmem] * (1 + len(parts)),
            out_specs=vmem,
            out_shape=packed,
            compiler_params=params(),
            name="add_packed",
        )(flag, keep, *parts)

    a_step = math.gcd(HEADS_A_STEP, half_heads)
    grid = (heads // a_step,)
    wide = pl.BlockSpec((row_count, a_step * width), lambda i, *_: (0, i))
    narrow = pl.BlockSpec((row_count, 128), lambda i, *_: (0, i))
    whole = pl.BlockSpec(packed.shape, lambda i, *_: (0, 0))
    full = jax.ShapeDtypeStruct((row_count, columns), BF16)
    full_f32 = jax.ShapeDtypeStruct((row_count, columns), F32)

    def scores(where, key_len, query_rows, key_rows, value_rows, *keys):
        return pl.pallas_call(
            functools.partial(scores_kernel, width, levels),
            grid_spec=pltpu.PrefetchScalarGridSpec(
                num_scalar_prefetch=2,
                grid=grid,
                in_specs=[wide] * (1 + levels + 1 + 1),
                out_specs=[wide] * levels + [narrow, wide],
            ),
            out_shape=[full] * levels + [jax.ShapeDtypeStruct((row_count, grid[0] * 128), F32), full_f32],
            compiler_params=params(),
            name="scores",
        )(where, key_len, query_rows, key_rows, *keys, value_rows)

    one = jnp.ones((1,), jnp.int32)
    far_keys = [moved(key_rows, turns[0])]
    keep, near = fenced(block_sums, where, key_len, key_rows, value_rows)
    near_keys = moved(after(key_rows, near), swaps)
    near_values = moved(after(value_rows, near), swaps)
    hops = [moved(add_packed(one, keep, near), steps[0])]
    far_keys += [moved(after(key_rows, near), turn) for turn in turns[1:]]
    hops.append(moved(add_packed(one, keep, after(near, far_keys[0]), *hops), steps[1]))
    held = [pair for pair in turns[0] if pair[0] < 2 and levels == 3]
    early = [pair for pair in turns[0] if pair not in held]
    first_values = [moved(after(value_rows, near_keys, *far_keys), early)]

    def last_hop(keep, parts, *operands):
        for pairs in steps[2:]:
            parts = [*parts, moved(add_packed(one, keep, *parts), pairs)]
        return parts[1:], scores(*operands), [moved(operands[4], held)] if held else []

    hops, (*weights, factors, base), rest = fenced(
        last_hop, keep, [near, *hops], where, key_len, query_rows, key_rows, value_rows, near_keys, *far_keys
    )
    first_values += rest
    far_values = [moved(after(value_rows, *hops), turn) for turn in turns[1:]]

    half_grid = grid[0] // 2
    half_f32 = jax.ShapeDtypeStruct((row_count, columns // 2), F32)

    def linear(own, where, linear_scale, query_rows, factors, base, weights, near_values, *parts):
        def at(i, where, scale):
            side = lax.rem(where[0], 2)
            return 0, (side if own else 1 - side) * half_grid + i

        chosen = pl.BlockSpec((row_count, a_step * width), at)
        return pl.pallas_call(
            functools.partial(linear_kernel, heads, width, own, len(parts), tokens),
            grid_spec=pltpu.PrefetchScalarGridSpec(
                num_scalar_prefetch=2,
                grid=(half_grid,),
                in_specs=[chosen, pl.BlockSpec((row_count, 128), at)] + [chosen] * 3 + [whole] * len(parts),
                out_specs=wide,
            ),
            out_shape=half_f32,
            compiler_params=params(),
            name="linear_own" if own else "linear_other",
        )(where, linear_scale, query_rows, factors, base, weights, near_values, *parts)

    operands = (where, linear_scale, query_rows, factors, base, weights[0], near_values)

    def last_exchange(flag, keep, near, hops, *operands):
        return moved(add_packed(flag, keep, *hops), swaps), linear(True, *operands, *hops, near)

    far, own = fenced(last_exchange, 1 - lax.rem(where, 2), keep, near, hops, *operands)
    other = linear(False, *operands, far)
    half = pl.BlockSpec((row_count, a_step * width), lambda i, *_: (0, lax.rem(i, half_grid)))
    return pl.pallas_call(
        functools.partial(finish_kernel, late, width),
        grid_spec=pltpu.PrefetchScalarGridSpec(
            num_scalar_prefetch=1,
            grid=grid,
            in_specs=[narrow, half, half] + [wide] * (late + len(first_values) + late - 1),
            out_specs=wide,
        ),
        out_shape=full,
        compiler_params=params(),
        name="finish",
    )(where, factors, own, other, *weights[1:], *first_values, *far_values)


def solution(mesh):
    return jax.shard_map(
        shards,
        mesh=mesh,
        in_specs=(
            P(("groups", "seq"), "head"),
            P(("groups", "seq"), "head"),
            P(("groups", "seq"), "head"),
            P("groups"),
            P("head"),
        ),
        out_specs=P(("groups", "seq"), "head"),
        check_vma=False,
    )
```

```python
import functools
import math

import jax
import jax.numpy as jnp
from jax import lax
from jax.experimental import pallas as pl
from jax.experimental.pallas import tpu as pltpu
from jax.sharding import PartitionSpec as P

CENTER = 1.125
TERMS = 3
HEADS_A_STEP = 4
VMEM_BYTES = 40 * 1024 * 1024
F32 = jnp.float32
BF16 = jnp.bfloat16


def feature(x):
    return jnp.where(x > 0.0, x + 1.0, jnp.exp(jnp.minimum(x, 0.0)))


def halves(x):
    high = x.astype(BF16)
    return high, (x - high.astype(F32)).astype(BF16)


def padded(count):
    return -(-count // 16) * 16


def store_packed(ref, main, sums):
    rows, extra = main.shape[0], sums.shape[0]
    ref[0:rows, :] = main.astype(BF16)
    for term in range(TERMS):
        part = sums.astype(BF16)
        sums = sums - part.astype(F32)
        ref[rows + term * extra : rows + (term + 1) * extra, :] = part


def packed_sums(ref, rows, extra):
    total = ref[rows : rows + extra, :].astype(F32)
    for term in range(1, TERMS):
        total = total + ref[rows + term * extra : rows + (term + 1) * extra, :].astype(F32)
    return total


def block_sums_kernel(heads, width, where, lengths, k_ref, v_ref, send_ref, keep_ref):
    half_heads = heads // 2
    me = where[0]
    side = lax.rem(me, 2)
    length = lengths[me]
    rows = half_heads * width
    extra = padded(half_heads)
    live = lax.broadcasted_iota(jnp.int32, (k_ref.shape[0], width), 0) < length

    def one_half(first, store):
        sums = []
        for i in range(half_heads):
            columns = pl.ds(pl.multiple_of((first + i) * width, width), width)
            mapped = jnp.where(live, feature(k_ref[:, columns].astype(F32)) - CENTER, 0.0)
            values = jnp.where(live, v_ref[:, columns].astype(F32), 0.0)
            sums.append(jnp.sum(values, axis=0, keepdims=True))
            high, low = halves(mapped)
            values = values.astype(BF16)
            store(
                i,
                lax.dot_general(
                    jnp.concatenate([high, low], axis=0),
                    jnp.concatenate([values, values], axis=0),
                    (((0,), (0,)), ((), ())),
                    preferred_element_type=F32,
                ),
            )
        sums += [jnp.zeros((1, width), F32)] * (extra - half_heads)
        return jnp.concatenate(sums, axis=0)

    def store_send(i, value):
        send_ref[i * width : (i + 1) * width, :] = value.astype(BF16)

    def store_keep(i, value):
        keep_ref[i * width : (i + 1) * width, :] = value

    sums = one_half((1 - side) * half_heads, store_send)
    for term in range(TERMS):
        part = sums.astype(BF16)
        sums = sums - part.astype(F32)
        send_ref[rows + term * extra : rows + (term + 1) * extra, :] = part
    keep_ref[rows : rows + extra, :] = one_half(side * half_heads, store_keep)


def add_packed_kernel(rows, extra, count, where, keep_ref, *refs):
    flag = where[0].astype(F32)
    main = keep_ref[0:rows, :] * flag
    sums = keep_ref[rows : rows + extra, :] * flag
    for ref in refs[:count]:
        main = main + ref[0:rows, :].astype(F32)
        sums = sums + packed_sums(ref, rows, extra)
    store_packed(refs[count], main, sums)


def partners(me, levels):
    if levels != 3:
        return [me] + [jnp.bitwise_xor(me, 1 << level) for level in range(levels)]
    pair = me // 2
    inner = lax.rem(pair + pair // 2, 2)
    return [me, jnp.bitwise_xor(me, 1), jnp.bitwise_xor(me, 2 + 2 * inner), jnp.bitwise_xor(me, 4 - 2 * inner)]


def exchanges(levels):
    count = 1 << levels
    if levels != 3:
        return [[(i, i ^ 1 << level) for i in range(count)] for level in range(1, levels)]
    cycle = [(0, 2), (2, 3), (3, 1), (1, 0)]
    return [
        [(2 * a + y, 2 * b + y) for a, b in cycle for y in (0, 1)],
        [(2 * b + y, 2 * a + y) for a, b in cycle for y in (0, 1)],
    ]


def scores_kernel(width, levels, where, lengths, q_ref, *refs):
    key_refs, refs = refs[: levels + 1], refs[levels + 1 :]
    value_ref, refs = refs[0], refs[1:]
    weight_refs, (factor_ref, base_ref) = refs[:levels], refs[levels:]
    row_count = q_ref.shape[0]
    a_step = q_ref.shape[1] // width
    column = lax.broadcasted_iota(jnp.int32, (row_count, row_count), 1)
    row = lax.broadcasted_iota(jnp.int32, (row_count, row_count), 0)
    allowed = [column < lengths[partner] for partner in partners(where[0], levels)]
    allowed[0] = allowed[0] & (column <= row)
    lane = lax.broadcasted_iota(jnp.int32, (row_count, 128), 1)
    factors = jnp.zeros((row_count, 128), F32)
    for h in range(a_step):
        at = slice(h * width, (h + 1) * width)
        queries = q_ref[:, at]
        peaks, totals, weights = [], [], []
        for which in range(levels + 1):
            s = lax.dot_general(
                queries, key_refs[which][:, at], (((1,), (1,)), ((), ())), preferred_element_type=F32
            ) * (1.0 / math.sqrt(width))
            s = jnp.where(allowed[which], s, -jnp.inf)
            peak = jnp.max(s, axis=1, keepdims=True)
            p = jnp.exp(s - peak).astype(BF16)
            peaks.append(peak)
            weights.append(p)
            totals.append(jnp.sum(p.astype(F32), axis=1, keepdims=True))
        peak = functools.reduce(jnp.maximum, peaks)
        shares = [jnp.exp(one - peak) for one in peaks]
        whole = functools.reduce(jnp.add, [a * b for a, b in zip(shares, totals)])
        shares = [share / whole for share in shares]
        base_ref[:, at] = shares[0] * jnp.dot(weights[0], value_ref[:, at], preferred_element_type=F32)
        for which in range(levels):
            weight_refs[which][:, at] = weights[which + 1]
            factors = jnp.where(lane == which * a_step + h, shares[which + 1], factors)
    factor_ref[...] = factors


def parts_kernel(width, counts, factor_ref, base_ref, *refs):
    weight_refs, value_refs, out_ref = refs[: len(counts)], refs[len(counts) : -1], refs[-1]
    a_step = base_ref.shape[1] // width
    for h in range(a_step):
        at = slice(h * width, (h + 1) * width)
        total = base_ref[:, at]
        first = 0
        for which, count in enumerate(counts):
            values = functools.reduce(jnp.add, [ref[:, at] for ref in value_refs[first : first + count]])
            first += count
            lane = which * a_step + h
            total = total + factor_ref[:, lane : lane + 1] * jnp.dot(
                weight_refs[which][:, at], values, preferred_element_type=F32
            )
        out_ref[:, at] = total


def linear_kernel(heads, width, own, parts, tokens, where, scale, q_ref, *refs):
    part_refs, out_ref = refs[:parts], refs[parts]
    side = lax.rem(where[0], 2)
    half_heads = heads // 2
    rows, extra = half_heads * width, padded(half_heads)
    start = (side if own else 1 - side) * half_heads
    flags = [1.0] * (parts - 1) + [side.astype(F32) if own else 1.0]
    sums = functools.reduce(
        jnp.add, [flag * packed_sums(ref, rows, extra) for flag, ref in zip(flags, part_refs)]
    )
    for h in range(half_heads):
        at = pl.ds(pl.multiple_of((start + h) * width, width), width)
        block = slice(h * width, (h + 1) * width)
        mapped = feature(q_ref[:, at].astype(F32))
        high, low = halves(mapped)
        if own:
            prefix = functools.reduce(
                jnp.add, [flag * ref[block, :].astype(F32) for flag, ref in zip(flags, part_refs)]
            )
            prefix, rest = halves(prefix)
        else:
            prefix = part_refs[0][block, :]
        linear = jnp.dot(
            jnp.concatenate([high, low], axis=1),
            jnp.concatenate([prefix, prefix], axis=0),
            preferred_element_type=F32,
        )
        if own:
            linear = linear + jnp.dot(high, rest, preferred_element_type=F32)
        linear = linear + jnp.sum(mapped, axis=1, keepdims=True) * (CENTER * sums[h : h + 1, :])
        out_ref[:, block] = linear * (scale[start + h] * (1.0 / (width * math.sqrt(tokens))))


def finish_kernel(heads, width, late, a_step, where, factor_ref, base_ref, own_ref, other_ref, *refs):
    weight_refs, value_refs, out_ref = refs[: late - 1], refs[late - 1 : -1], refs[-1]
    side = lax.rem(where[0], 2)
    half_heads = heads // 2
    for own, linear_ref in ((True, own_ref), (False, other_ref)):
        start = (side if own else 1 - side) * half_heads
        for h in range(half_heads):
            at = pl.ds(pl.multiple_of((start + h) * width, width), width)
            total = base_ref[:, at] + linear_ref[:, h * width : (h + 1) * width]
            column = pl.ds(pl.multiple_of((start + h) // a_step * 128, 128), 128)
            factors = factor_ref[:, column]
            for which in range(late - 1):
                lane = (which + 2) * a_step + h % a_step
                total = total + factors[:, lane : lane + 1] * jnp.dot(
                    weight_refs[which][:, at], value_refs[which][:, at], preferred_element_type=F32
                )
            out_ref[:, at] = total.astype(BF16)


def params():
    return pltpu.CompilerParams(vmem_limit_bytes=VMEM_BYTES)


def shards(query_rows, key_rows, value_rows, key_len, linear_scale):
    row_count, columns = query_rows.shape
    heads = linear_scale.shape[0]
    width = columns // heads
    half_heads = heads // 2
    count = lax.axis_size("seq")
    levels = count.bit_length() - 1
    late = levels - 1
    me = lax.axis_index("seq").astype(jnp.int32)
    where = me.reshape(1)
    tokens = row_count * count
    rows, extra = half_heads * width, padded(half_heads)
    packed = jax.ShapeDtypeStruct((rows + TERMS * extra, width), BF16)
    smem = pl.BlockSpec(memory_space=pltpu.SMEM)
    vmem = pl.BlockSpec(memory_space=pltpu.VMEM)

    pairs_of_blocks = count // 2
    if pairs_of_blocks <= 4:
        steps = [[(z, z + 1)] for z in range(pairs_of_blocks - 1)]
    else:
        steps = [
            [(z, z + (1 << d)) for z in range(pairs_of_blocks - (1 << d))]
            for d in range((pairs_of_blocks - 1).bit_length())
        ]
    steps = [[(2 * a + y, 2 * b + y) for a, b in pairs for y in (0, 1)] for pairs in steps]
    swaps = [(i, i ^ 1) for i in range(count)]
    turns = exchanges(levels)

    def moved(x, pairs):
        return lax.ppermute(x, "seq", pairs)

    def after(x, *done):
        return lax.optimization_barrier((x, *done))[0]

    def fenced(run, *operands):
        shapes = jax.eval_shape(run, *operands)

        def nothing(*_):
            return jax.tree.map(lambda leaf: jnp.zeros(leaf.shape, leaf.dtype), shapes)

        return lax.cond(key_len[0] > 0, run, nothing, *operands)

    def block_sums(where, key_len, key_rows, value_rows):
        send, keep = pl.pallas_call(
            functools.partial(block_sums_kernel, heads, width),
            in_specs=[smem, smem, vmem, vmem],
            out_specs=[vmem, vmem],
            out_shape=[packed, jax.ShapeDtypeStruct((rows + extra, width), F32)],
            compiler_params=params(),
            name="block_sums",
        )(where, key_len, key_rows, value_rows)
        return keep, moved(send, swaps)

    def add_packed(flag, keep, *parts):
        return pl.pallas_call(
            functools.partial(add_packed_kernel, rows, extra, len(parts)),
            in_specs=[smem] + [vmem] * (1 + len(parts)),
            out_specs=vmem,
            out_shape=packed,
            compiler_params=params(),
            name="add_packed",
        )(flag, keep, *parts)

    a_step = math.gcd(HEADS_A_STEP, half_heads)
    grid = (heads // a_step,)
    wide = pl.BlockSpec((row_count, a_step * width), lambda i, *_: (0, i))
    narrow = pl.BlockSpec((row_count, 128), lambda i, *_: (0, i))
    whole = pl.BlockSpec(packed.shape, lambda i, *_: (0, 0))
    full = jax.ShapeDtypeStruct((row_count, columns), BF16)
    full_f32 = jax.ShapeDtypeStruct((row_count, columns), F32)

    def scores(where, key_len, query_rows, key_rows, value_rows, *keys):
        return pl.pallas_call(
            functools.partial(scores_kernel, width, levels),
            grid_spec=pltpu.PrefetchScalarGridSpec(
                num_scalar_prefetch=2,
                grid=grid,
                in_specs=[wide] * (1 + levels + 1 + 1),
                out_specs=[wide] * levels + [narrow, wide],
            ),
            out_shape=[full] * levels + [jax.ShapeDtypeStruct((row_count, grid[0] * 128), F32), full_f32],
            compiler_params=params(),
            name="scores",
        )(where, key_len, query_rows, key_rows, *keys, value_rows)

    one = jnp.ones((1,), jnp.int32)
    far_keys = [moved(key_rows, turns[0])]
    keep, near = fenced(block_sums, where, key_len, key_rows, value_rows)
    near_keys = moved(after(key_rows, near), swaps)
    hops = [moved(add_packed(one, keep, near), steps[0])]
    far_keys += [moved(after(key_rows, near), turn) for turn in turns[1:]]
    hops.append(moved(add_packed(one, keep, after(near, far_keys[0]), *hops), steps[1]))
    held = [pair for pair in turns[0] if pair[0] < 2 and levels == 3]
    early = [pair for pair in turns[0] if pair not in held]
    first_values = [moved(after(value_rows, near_keys), early)]
    near_values = moved(after(value_rows, near_keys, *far_keys), swaps)
    if held:
        first_values.append(moved(after(value_rows, near_keys, *far_keys), held))

    def last_hop(keep, parts, *operands):
        for pairs in steps[2:]:
            parts = [*parts, moved(add_packed(one, keep, *parts), pairs)]
        return parts[1:], scores(*operands)

    hops, (*weights, factors, base) = fenced(
        last_hop, keep, [near, *hops], where, key_len, query_rows, key_rows, value_rows, near_keys, *far_keys
    )
    far_values = [moved(after(value_rows, *hops), turn) for turn in turns[1:]]

    far = moved(add_packed(1 - lax.rem(where, 2), keep, *hops), swaps)
    def linear(own, *parts):
        return pl.pallas_call(
            functools.partial(linear_kernel, heads, width, own, len(parts), tokens),
            in_specs=[smem, smem] + [vmem] * (1 + len(parts)),
            out_specs=vmem,
            out_shape=jax.ShapeDtypeStruct((row_count, columns // 2), F32),
            compiler_params=params(),
            name="linear_own" if own else "linear_other",
        )(where, linear_scale, query_rows, *parts)

    own = linear(True, *hops, after(near, first_values[0]))
    base = pl.pallas_call(
        functools.partial(parts_kernel, width, [1, len(first_values)]),
        grid=grid,
        in_specs=[narrow] + [wide] * (1 + 2 + 1 + len(first_values)),
        out_specs=wide,
        out_shape=full_f32,
        compiler_params=params(),
        name="parts",
    )(factors, after(base, own), *weights[:2], near_values, *first_values)

    other = linear(False, far)
    return pl.pallas_call(
        functools.partial(finish_kernel, heads, width, late, a_step),
        in_specs=[smem] + [vmem] * (4 + 2 * (late - 1)),
        out_specs=vmem,
        out_shape=full,
        compiler_params=params(),
        name="finish",
    )(where, factors, base, own, other, *weights[2:], *far_values)


def solution(mesh):
    return jax.shard_map(
        shards,
        mesh=mesh,
        in_specs=(
            P(("groups", "seq"), "head"),
            P(("groups", "seq"), "head"),
            P(("groups", "seq"), "head"),
            P("groups"),
            P("head"),
        ),
        out_specs=P(("groups", "seq"), "head"),
        check_vma=False,
    )
```

```python
import functools
import math

import jax
import jax.numpy as jnp
from jax import lax
from jax.experimental import pallas as pl
from jax.experimental.pallas import tpu as pltpu
from jax.sharding import PartitionSpec as P

CENTER = 1.125
TERMS = 3
HEADS_A_STEP = 4
VMEM_BYTES = 40 * 1024 * 1024
F32 = jnp.float32
BF16 = jnp.bfloat16


def feature(x):
    return jnp.where(x > 0.0, x + 1.0, jnp.exp(jnp.minimum(x, 0.0)))


def halves(x):
    high = x.astype(BF16)
    return high, (x - high.astype(F32)).astype(BF16)


def padded(count):
    return -(-count // 16) * 16


def store_packed(ref, main, sums):
    rows, extra = main.shape[0], sums.shape[0]
    ref[0:rows, :] = main.astype(BF16)
    for term in range(TERMS):
        part = sums.astype(BF16)
        sums = sums - part.astype(F32)
        ref[rows + term * extra : rows + (term + 1) * extra, :] = part


def packed_sums(ref, rows, extra):
    total = ref[rows : rows + extra, :].astype(F32)
    for term in range(1, TERMS):
        total = total + ref[rows + term * extra : rows + (term + 1) * extra, :].astype(F32)
    return total


def block_sums_kernel(heads, width, where, lengths, k_ref, v_ref, send_ref, keep_ref):
    half_heads = heads // 2
    me = where[0]
    side = lax.rem(me, 2)
    length = lengths[me]
    rows = half_heads * width
    extra = padded(half_heads)
    live = lax.broadcasted_iota(jnp.int32, (k_ref.shape[0], width), 0) < length

    def one_half(first, store):
        sums = []
        for i in range(half_heads):
            columns = pl.ds(pl.multiple_of((first + i) * width, width), width)
            mapped = jnp.where(live, feature(k_ref[:, columns].astype(F32)) - CENTER, 0.0)
            values = jnp.where(live, v_ref[:, columns].astype(F32), 0.0)
            sums.append(jnp.sum(values, axis=0, keepdims=True))
            high, low = halves(mapped)
            values = values.astype(BF16)
            store(
                i,
                lax.dot_general(
                    jnp.concatenate([high, low], axis=0),
                    jnp.concatenate([values, values], axis=0),
                    (((0,), (0,)), ((), ())),
                    preferred_element_type=F32,
                ),
            )
        sums += [jnp.zeros((1, width), F32)] * (extra - half_heads)
        return jnp.concatenate(sums, axis=0)

    def store_send(i, value):
        send_ref[i * width : (i + 1) * width, :] = value.astype(BF16)

    def store_keep(i, value):
        keep_ref[i * width : (i + 1) * width, :] = value

    sums = one_half((1 - side) * half_heads, store_send)
    for term in range(TERMS):
        part = sums.astype(BF16)
        sums = sums - part.astype(F32)
        send_ref[rows + term * extra : rows + (term + 1) * extra, :] = part
    keep_ref[rows : rows + extra, :] = one_half(side * half_heads, store_keep)


def add_packed_kernel(rows, extra, count, where, keep_ref, *refs):
    flag = where[0].astype(F32)
    main = keep_ref[0:rows, :] * flag
    sums = keep_ref[rows : rows + extra, :] * flag
    for ref in refs[:count]:
        main = main + ref[0:rows, :].astype(F32)
        sums = sums + packed_sums(ref, rows, extra)
    store_packed(refs[count], main, sums)


def partners(me, levels):
    if levels != 3:
        return [me] + [jnp.bitwise_xor(me, 1 << level) for level in range(levels)]
    pair = me // 2
    inner = lax.rem(pair + pair // 2, 2)
    return [me, jnp.bitwise_xor(me, 1), jnp.bitwise_xor(me, 2 + 2 * inner), jnp.bitwise_xor(me, 4 - 2 * inner)]


def exchanges(levels):
    count = 1 << levels
    if levels != 3:
        return [[(i, i ^ 1 << level) for i in range(count)] for level in range(1, levels)]
    cycle = [(0, 2), (2, 3), (3, 1), (1, 0)]
    return [
        [(2 * a + y, 2 * b + y) for a, b in cycle for y in (0, 1)],
        [(2 * b + y, 2 * a + y) for a, b in cycle for y in (0, 1)],
    ]


def scores_kernel(width, levels, where, lengths, q_ref, *refs):
    key_refs, refs = refs[: levels + 1], refs[levels + 1 :]
    value_ref, refs = refs[0], refs[1:]
    weight_refs, (factor_ref, base_ref) = refs[:levels], refs[levels:]
    row_count = q_ref.shape[0]
    a_step = q_ref.shape[1] // width
    column = lax.broadcasted_iota(jnp.int32, (row_count, row_count), 1)
    row = lax.broadcasted_iota(jnp.int32, (row_count, row_count), 0)
    allowed = [column < lengths[partner] for partner in partners(where[0], levels)]
    allowed[0] = allowed[0] & (column <= row)
    lane = lax.broadcasted_iota(jnp.int32, (row_count, 128), 1)
    factors = jnp.zeros((row_count, 128), F32)
    for h in range(a_step):
        at = slice(h * width, (h + 1) * width)
        queries = q_ref[:, at]
        peaks, totals, weights = [], [], []
        for which in range(levels + 1):
            s = lax.dot_general(
                queries, key_refs[which][:, at], (((1,), (1,)), ((), ())), preferred_element_type=F32
            ) * (1.0 / math.sqrt(width))
            s = jnp.where(allowed[which], s, -jnp.inf)
            peak = jnp.max(s, axis=1, keepdims=True)
            p = jnp.exp(s - peak).astype(BF16)
            peaks.append(peak)
            weights.append(p)
            totals.append(jnp.sum(p.astype(F32), axis=1, keepdims=True))
        peak = functools.reduce(jnp.maximum, peaks)
        shares = [jnp.exp(one - peak) for one in peaks]
        whole = functools.reduce(jnp.add, [a * b for a, b in zip(shares, totals)])
        shares = [share / whole for share in shares]
        base_ref[:, at] = shares[0] * jnp.dot(weights[0], value_ref[:, at], preferred_element_type=F32)
        for which in range(levels):
            weight_refs[which][:, at] = weights[which + 1]
            factors = jnp.where(lane == which * a_step + h, shares[which + 1], factors)
    factor_ref[...] = factors


def parts_kernel(width, counts, factor_ref, base_ref, *refs):
    weight_refs, value_refs, out_ref = refs[: len(counts)], refs[len(counts) : -1], refs[-1]
    a_step = base_ref.shape[1] // width
    for h in range(a_step):
        at = slice(h * width, (h + 1) * width)
        total = base_ref[:, at]
        first = 0
        for which, count in enumerate(counts):
            values = functools.reduce(jnp.add, [ref[:, at] for ref in value_refs[first : first + count]])
            first += count
            lane = which * a_step + h
            total = total + factor_ref[:, lane : lane + 1] * jnp.dot(
                weight_refs[which][:, at], values, preferred_element_type=F32
            )
        out_ref[:, at] = total


def linear_kernel(heads, width, own, parts, tokens, where, scale, q_ref, *refs):
    part_refs, out_ref = refs[:parts], refs[parts]
    side = lax.rem(where[0], 2)
    half_heads = heads // 2
    rows, extra = half_heads * width, padded(half_heads)
    start = (side if own else 1 - side) * half_heads
    flags = [1.0] * (parts - 1) + [side.astype(F32) if own else 1.0]
    sums = functools.reduce(
        jnp.add, [flag * packed_sums(ref, rows, extra) for flag, ref in zip(flags, part_refs)]
    )
    for h in range(half_heads):
        at = pl.ds(pl.multiple_of((start + h) * width, width), width)
        block = slice(h * width, (h + 1) * width)
        mapped = feature(q_ref[:, at].astype(F32))
        high, low = halves(mapped)
        if own:
            prefix = functools.reduce(
                jnp.add, [flag * ref[block, :].astype(F32) for flag, ref in zip(flags, part_refs)]
            )
            prefix, rest = halves(prefix)
        else:
            prefix = part_refs[0][block, :]
        linear = jnp.dot(
            jnp.concatenate([high, low], axis=1),
            jnp.concatenate([prefix, prefix], axis=0),
            preferred_element_type=F32,
        )
        if own:
            linear = linear + jnp.dot(high, rest, preferred_element_type=F32)
        linear = linear + jnp.sum(mapped, axis=1, keepdims=True) * (CENTER * sums[h : h + 1, :])
        out_ref[:, block] = linear * (scale[start + h] * (1.0 / (width * math.sqrt(tokens))))


def finish_kernel(heads, width, late, a_step, where, factor_ref, base_ref, own_ref, other_ref, *refs):
    weight_refs, value_refs, out_ref = refs[: late - 1], refs[late - 1 : -1], refs[-1]
    side = lax.rem(where[0], 2)
    half_heads = heads // 2
    for own, linear_ref in ((True, own_ref), (False, other_ref)):
        start = (side if own else 1 - side) * half_heads
        for h in range(half_heads):
            at = pl.ds(pl.multiple_of((start + h) * width, width), width)
            total = base_ref[:, at] + linear_ref[:, h * width : (h + 1) * width]
            column = pl.ds(pl.multiple_of((start + h) // a_step * 128, 128), 128)
            factors = factor_ref[:, column]
            for which in range(late - 1):
                lane = (which + 2) * a_step + h % a_step
                total = total + factors[:, lane : lane + 1] * jnp.dot(
                    weight_refs[which][:, at], value_refs[which][:, at], preferred_element_type=F32
                )
            out_ref[:, at] = total.astype(BF16)


def params():
    return pltpu.CompilerParams(vmem_limit_bytes=VMEM_BYTES)


def shards(query_rows, key_rows, value_rows, key_len, linear_scale):
    row_count, columns = query_rows.shape
    heads = linear_scale.shape[0]
    width = columns // heads
    half_heads = heads // 2
    count = lax.axis_size("seq")
    levels = count.bit_length() - 1
    late = levels - 1
    me = lax.axis_index("seq").astype(jnp.int32)
    where = me.reshape(1)
    tokens = row_count * count
    rows, extra = half_heads * width, padded(half_heads)
    packed = jax.ShapeDtypeStruct((rows + TERMS * extra, width), BF16)
    smem = pl.BlockSpec(memory_space=pltpu.SMEM)
    vmem = pl.BlockSpec(memory_space=pltpu.VMEM)

    pairs_of_blocks = count // 2
    if pairs_of_blocks <= 4:
        steps = [[(z, z + 1)] for z in range(pairs_of_blocks - 1)]
    else:
        steps = [
            [(z, z + (1 << d)) for z in range(pairs_of_blocks - (1 << d))]
            for d in range((pairs_of_blocks - 1).bit_length())
        ]
    steps = [[(2 * a + y, 2 * b + y) for a, b in pairs for y in (0, 1)] for pairs in steps]
    swaps = [(i, i ^ 1) for i in range(count)]
    turns = exchanges(levels)

    def moved(x, pairs):
        return lax.ppermute(x, "seq", pairs)

    def after(x, *done):
        return lax.optimization_barrier((x, *done))[0]

    def fenced(run, *operands):
        shapes = jax.eval_shape(run, *operands)

        def nothing(*_):
            return jax.tree.map(lambda leaf: jnp.zeros(leaf.shape, leaf.dtype), shapes)

        return lax.cond(key_len[0] > 0, run, nothing, *operands)

    def block_sums(where, key_len, key_rows, value_rows):
        send, keep = pl.pallas_call(
            functools.partial(block_sums_kernel, heads, width),
            in_specs=[smem, smem, vmem, vmem],
            out_specs=[vmem, vmem],
            out_shape=[packed, jax.ShapeDtypeStruct((rows + extra, width), F32)],
            compiler_params=params(),
            name="block_sums",
        )(where, key_len, key_rows, value_rows)
        return keep, moved(send, swaps)

    def add_packed(flag, keep, *parts):
        return pl.pallas_call(
            functools.partial(add_packed_kernel, rows, extra, len(parts)),
            in_specs=[smem] + [vmem] * (1 + len(parts)),
            out_specs=vmem,
            out_shape=packed,
            compiler_params=params(),
            name="add_packed",
        )(flag, keep, *parts)

    a_step = math.gcd(HEADS_A_STEP, half_heads)
    grid = (heads // a_step,)
    wide = pl.BlockSpec((row_count, a_step * width), lambda i, *_: (0, i))
    narrow = pl.BlockSpec((row_count, 128), lambda i, *_: (0, i))
    whole = pl.BlockSpec(packed.shape, lambda i, *_: (0, 0))
    full = jax.ShapeDtypeStruct((row_count, columns), BF16)
    full_f32 = jax.ShapeDtypeStruct((row_count, columns), F32)

    def scores(where, key_len, query_rows, key_rows, value_rows, *keys):
        return pl.pallas_call(
            functools.partial(scores_kernel, width, levels),
            grid_spec=pltpu.PrefetchScalarGridSpec(
                num_scalar_prefetch=2,
                grid=grid,
                in_specs=[wide] * (1 + levels + 1 + 1),
                out_specs=[wide] * levels + [narrow, wide],
            ),
            out_shape=[full] * levels + [jax.ShapeDtypeStruct((row_count, grid[0] * 128), F32), full_f32],
            compiler_params=params(),
            name="scores",
        )(where, key_len, query_rows, key_rows, *keys, value_rows)

    one = jnp.ones((1,), jnp.int32)
    far_keys = [moved(key_rows, turns[0])]
    keep, near = fenced(block_sums, where, key_len, key_rows, value_rows)
    near_keys = moved(after(key_rows, near), swaps)
    hops = [moved(add_packed(one, keep, near), steps[0])]
    far_keys += [moved(after(key_rows, near), turn) for turn in turns[1:]]
    hops.append(moved(add_packed(one, keep, after(near, far_keys[0]), *hops), steps[1]))
    held = [pair for pair in turns[0] if pair[0] < 2 and levels == 3]
    early = [pair for pair in turns[0] if pair not in held]
    first_values = [moved(after(value_rows, near_keys), early)]
    near_values = moved(after(value_rows, near_keys, *far_keys), swaps)
    if held:
        first_values.append(moved(after(value_rows, near_keys, *far_keys), held))
    far_values = [moved(after(value_rows, hops[1]), turn) for turn in turns[1:]]

    def last_hop(keep, parts, *operands):
        for pairs in steps[2:]:
            parts = [*parts, moved(add_packed(one, keep, *parts), pairs)]
        return parts[1:], scores(*operands)

    hops, (*weights, factors, base) = fenced(
        last_hop, keep, [near, *hops], where, key_len, query_rows, key_rows, value_rows, near_keys, *far_keys
    )

    far = moved(add_packed(1 - lax.rem(where, 2), keep, *hops), swaps)

    def linear(own, *parts):
        return pl.pallas_call(
            functools.partial(linear_kernel, heads, width, own, len(parts), tokens),
            in_specs=[smem, smem] + [vmem] * (1 + len(parts)),
            out_specs=vmem,
            out_shape=jax.ShapeDtypeStruct((row_count, columns // 2), F32),
            compiler_params=params(),
            name="linear_own" if own else "linear_other",
        )(where, linear_scale, query_rows, *parts)

    own = linear(True, *hops, after(near, first_values[0]))
    base = pl.pallas_call(
        functools.partial(parts_kernel, width, [1, len(first_values)]),
        grid=grid,
        in_specs=[narrow] + [wide] * (1 + 2 + 1 + len(first_values)),
        out_specs=wide,
        out_shape=full_f32,
        compiler_params=params(),
        name="parts",
    )(factors, after(base, own), *weights[:2], near_values, *first_values)

    other = linear(False, far)
    return pl.pallas_call(
        functools.partial(finish_kernel, heads, width, late, a_step),
        in_specs=[smem] + [vmem] * (4 + 2 * (late - 1)),
        out_specs=vmem,
        out_shape=full,
        compiler_params=params(),
        name="finish",
    )(where, factors, base, own, other, *weights[2:], *far_values)


def solution(mesh):
    return jax.shard_map(
        shards,
        mesh=mesh,
        in_specs=(
            P(("groups", "seq"), "head"),
            P(("groups", "seq"), "head"),
            P(("groups", "seq"), "head"),
            P("groups"),
            P("head"),
        ),
        out_specs=P(("groups", "seq"), "head"),
        check_vma=False,
    )
```

```python
import functools
import math

import jax
import jax.numpy as jnp
from jax import lax
from jax.experimental import pallas as pl
from jax.experimental.pallas import tpu as pltpu
from jax.sharding import PartitionSpec as P

CENTER = 1.125
TERMS = 3
HEADS_A_STEP = 4
VMEM_BYTES = 40 * 1024 * 1024
F32 = jnp.float32
BF16 = jnp.bfloat16


def feature(x):
    return jnp.where(x > 0.0, x + 1.0, jnp.exp(jnp.minimum(x, 0.0)))


def halves(x):
    high = x.astype(BF16)
    return high, (x - high.astype(F32)).astype(BF16)


def padded(count):
    return -(-count // 16) * 16


def store_packed(ref, main, sums):
    rows = main.shape[0]
    ref[0:rows, :] = main.astype(BF16)
    store_sums(ref, rows, sums)


def store_sums(ref, rows, sums):
    extra = sums.shape[0]
    for term in range(TERMS):
        part = sums.astype(BF16)
        sums = sums - part.astype(F32)
        ref[rows + term * extra : rows + (term + 1) * extra, :] = part


def packed_sums(ref, rows, extra):
    total = ref[rows : rows + extra, :].astype(F32)
    for term in range(1, TERMS):
        total = total + ref[rows + term * extra : rows + (term + 1) * extra, :].astype(F32)
    return total


def block_sums_kernel(heads, width, sent, where, lengths, k_ref, v_ref, out_ref):
    half_heads = heads // 2
    me = where[0]
    side = lax.rem(me, 2)
    length = lengths[me]
    rows = half_heads * width
    extra = padded(half_heads)
    first = (1 - side if sent else side) * half_heads
    live = lax.broadcasted_iota(jnp.int32, (k_ref.shape[0], width), 0) < length
    sums = []
    for i in range(half_heads):
        columns = pl.ds(pl.multiple_of((first + i) * width, width), width)
        mapped = jnp.where(live, feature(k_ref[:, columns].astype(F32)) - CENTER, 0.0)
        values = jnp.where(live, v_ref[:, columns].astype(F32), 0.0)
        sums.append(jnp.sum(values, axis=0, keepdims=True))
        high, low = halves(mapped)
        values = values.astype(BF16)
        out_ref[i * width : (i + 1) * width, :] = lax.dot_general(
            jnp.concatenate([high, low], axis=0),
            jnp.concatenate([values, values], axis=0),
            (((0,), (0,)), ((), ())),
            preferred_element_type=F32,
        ).astype(out_ref.dtype)
    sums = jnp.concatenate(sums + [jnp.zeros((1, width), F32)] * (extra - half_heads), axis=0)
    if sent:
        store_sums(out_ref, rows, sums)
    else:
        out_ref[rows : rows + extra, :] = sums


def add_packed_kernel(rows, extra, count, where, keep_ref, *refs):
    flag = where[0].astype(F32)
    main = keep_ref[0:rows, :] * flag
    sums = keep_ref[rows : rows + extra, :] * flag
    for ref in refs[:count]:
        main = main + ref[0:rows, :].astype(F32)
        sums = sums + packed_sums(ref, rows, extra)
    store_packed(refs[count], main, sums)


def partners(me, levels):
    if levels != 3:
        return [me] + [jnp.bitwise_xor(me, 1 << level) for level in range(levels)]
    pair = me // 2
    inner = lax.rem(pair + pair // 2, 2)
    return [me, jnp.bitwise_xor(me, 1), jnp.bitwise_xor(me, 2 + 2 * inner), jnp.bitwise_xor(me, 4 - 2 * inner)]


def exchanges(levels):
    count = 1 << levels
    if levels != 3:
        return [[(i, i ^ 1 << level) for i in range(count)] for level in range(1, levels)]
    cycle = [(0, 2), (2, 3), (3, 1), (1, 0)]
    return [
        [(2 * a + y, 2 * b + y) for a, b in cycle for y in (0, 1)],
        [(2 * b + y, 2 * a + y) for a, b in cycle for y in (0, 1)],
    ]


def scores_kernel(width, levels, where, lengths, q_ref, *refs):
    key_refs, refs = refs[: levels + 1], refs[levels + 1 :]
    value_ref, refs = refs[0], refs[1:]
    weight_refs, (factor_ref, base_ref) = refs[:levels], refs[levels:]
    row_count = q_ref.shape[0]
    a_step = q_ref.shape[1] // width
    column = lax.broadcasted_iota(jnp.int32, (row_count, row_count), 1)
    row = lax.broadcasted_iota(jnp.int32, (row_count, row_count), 0)
    allowed = [column < lengths[partner] for partner in partners(where[0], levels)]
    allowed[0] = allowed[0] & (column <= row)
    lane = lax.broadcasted_iota(jnp.int32, (row_count, 128), 1)
    factors = jnp.zeros((row_count, 128), F32)
    for h in range(a_step):
        at = slice(h * width, (h + 1) * width)
        queries = q_ref[:, at]
        peaks, totals, weights = [], [], []
        for which in range(levels + 1):
            s = lax.dot_general(
                queries, key_refs[which][:, at], (((1,), (1,)), ((), ())), preferred_element_type=F32
            ) * (1.0 / math.sqrt(width))
            s = jnp.where(allowed[which], s, -jnp.inf)
            peak = jnp.max(s, axis=1, keepdims=True)
            p = jnp.exp(s - peak).astype(BF16)
            peaks.append(peak)
            weights.append(p)
            totals.append(jnp.sum(p.astype(F32), axis=1, keepdims=True))
        peak = functools.reduce(jnp.maximum, peaks)
        shares = [jnp.exp(one - peak) for one in peaks]
        whole = functools.reduce(jnp.add, [a * b for a, b in zip(shares, totals)])
        shares = [share / whole for share in shares]
        base_ref[:, at] = shares[0] * jnp.dot(weights[0], value_ref[:, at], preferred_element_type=F32)
        for which in range(levels):
            weight_refs[which][:, at] = weights[which + 1]
            factors = jnp.where(lane == which * a_step + h, shares[which + 1], factors)
    factor_ref[...] = factors


def parts_kernel(width, counts, passed, factor_ref, base_ref, *refs):
    weight_refs, refs = refs[: len(counts)], refs[len(counts) :]
    last = len(refs) - 1 - 2 * passed
    value_refs, out_ref = refs[:last], refs[last + passed]
    for source, target in zip(refs[last : last + passed], refs[last + passed + 1 :]):
        target[...] = source[...]
    a_step = base_ref.shape[1] // width
    for h in range(a_step):
        at = slice(h * width, (h + 1) * width)
        total = base_ref[:, at]
        first = 0
        for which, count in enumerate(counts):
            values = functools.reduce(jnp.add, [ref[:, at] for ref in value_refs[first : first + count]])
            first += count
            lane = which * a_step + h
            total = total + factor_ref[:, lane : lane + 1] * jnp.dot(
                weight_refs[which][:, at], values, preferred_element_type=F32
            )
        out_ref[:, at] = total


def linear_kernel(heads, width, own, parts, tokens, where, scale, q_ref, *refs):
    part_refs, out_ref = refs[:parts], refs[parts]
    side = lax.rem(where[0], 2)
    half_heads = heads // 2
    rows, extra = half_heads * width, padded(half_heads)
    start = (side if own else 1 - side) * half_heads
    flags = [1.0] * (parts - 1) + [side.astype(F32) if own else 1.0]
    sums = functools.reduce(
        jnp.add, [flag * packed_sums(ref, rows, extra) for flag, ref in zip(flags, part_refs)]
    )
    for h in range(half_heads):
        at = pl.ds(pl.multiple_of((start + h) * width, width), width)
        block = slice(h * width, (h + 1) * width)
        mapped = feature(q_ref[:, at].astype(F32))
        high, low = halves(mapped)
        if own:
            prefix = functools.reduce(
                jnp.add, [flag * ref[block, :].astype(F32) for flag, ref in zip(flags, part_refs)]
            )
            prefix, rest = halves(prefix)
        else:
            prefix = part_refs[0][block, :]
        linear = jnp.dot(
            jnp.concatenate([high, low], axis=1),
            jnp.concatenate([prefix, prefix], axis=0),
            preferred_element_type=F32,
        )
        if own:
            linear = linear + jnp.dot(high, rest, preferred_element_type=F32)
        linear = linear + jnp.sum(mapped, axis=1, keepdims=True) * (CENTER * sums[h : h + 1, :])
        out_ref[:, block] = linear * (scale[start + h] * (1.0 / (width * math.sqrt(tokens))))


def finish_kernel(heads, width, late, a_step, where, factor_ref, base_ref, own_ref, other_ref, *refs):
    weight_refs, value_refs, out_ref = refs[: late - 1], refs[late - 1 : -1], refs[-1]
    side = lax.rem(where[0], 2)
    half_heads = heads // 2
    for own, linear_ref in ((True, own_ref), (False, other_ref)):
        start = (side if own else 1 - side) * half_heads
        for h in range(half_heads):
            at = pl.ds(pl.multiple_of((start + h) * width, width), width)
            total = base_ref[:, at] + linear_ref[:, h * width : (h + 1) * width]
            column = pl.ds(pl.multiple_of((start + h) // a_step * 128, 128), 128)
            factors = factor_ref[:, column]
            for which in range(late - 1):
                lane = (which + 2) * a_step + h % a_step
                total = total + factors[:, lane : lane + 1] * jnp.dot(
                    weight_refs[which][:, at], value_refs[which][:, at], preferred_element_type=F32
                )
            out_ref[:, at] = total.astype(BF16)


def params():
    return pltpu.CompilerParams(vmem_limit_bytes=VMEM_BYTES)


def shards(query_rows, key_rows, value_rows, key_len, linear_scale):
    row_count, columns = query_rows.shape
    heads = linear_scale.shape[0]
    width = columns // heads
    half_heads = heads // 2
    count = lax.axis_size("seq")
    levels = count.bit_length() - 1
    late = levels - 1
    me = lax.axis_index("seq").astype(jnp.int32)
    where = me.reshape(1)
    tokens = row_count * count
    rows, extra = half_heads * width, padded(half_heads)
    packed = jax.ShapeDtypeStruct((rows + TERMS * extra, width), BF16)
    smem = pl.BlockSpec(memory_space=pltpu.SMEM)
    vmem = pl.BlockSpec(memory_space=pltpu.VMEM)

    pairs_of_blocks = count // 2
    if pairs_of_blocks <= 4:
        steps = [[(z, z + 1)] for z in range(pairs_of_blocks - 1)]
    else:
        steps = [
            [(z, z + (1 << d)) for z in range(pairs_of_blocks - (1 << d))]
            for d in range((pairs_of_blocks - 1).bit_length())
        ]
    steps = [[(2 * a + y, 2 * b + y) for a, b in pairs for y in (0, 1)] for pairs in steps]
    swaps = [(i, i ^ 1) for i in range(count)]
    turns = exchanges(levels)

    def moved(x, pairs):
        return lax.ppermute(x, "seq", pairs)

    def after(x, *done):
        return lax.optimization_barrier((x, *done))[0]

    def fenced(run, *operands):
        shapes = jax.eval_shape(run, *operands)

        def nothing(*_):
            return jax.tree.map(lambda leaf: jnp.zeros(leaf.shape, leaf.dtype), shapes)

        return lax.cond(key_len[0] > 0, run, nothing, *operands)

    one = jnp.ones((1,), jnp.int32)

    def block_sums(where, key_len, key_rows, value_rows):
        def half(sent, shape):
            return pl.pallas_call(
                functools.partial(block_sums_kernel, heads, width, sent),
                in_specs=[smem, smem, vmem, vmem],
                out_specs=vmem,
                out_shape=shape,
                compiler_params=params(),
                name="sums_sent" if sent else "sums_kept",
            )(where, key_len, key_rows, value_rows)

        near = moved(half(True, packed), swaps)
        keep = half(False, jax.ShapeDtypeStruct((rows + extra, width), F32))
        return keep, near, add_packed(one, keep, near)

    def add_packed(flag, keep, *parts):
        return pl.pallas_call(
            functools.partial(add_packed_kernel, rows, extra, len(parts)),
            in_specs=[smem] + [vmem] * (1 + len(parts)),
            out_specs=vmem,
            out_shape=packed,
            compiler_params=params(),
            name="add_packed",
        )(flag, keep, *parts)

    a_step = math.gcd(HEADS_A_STEP, half_heads)
    grid = (heads // a_step,)
    wide = pl.BlockSpec((row_count, a_step * width), lambda i, *_: (0, i))
    narrow = pl.BlockSpec((row_count, 128), lambda i, *_: (0, i))
    whole = pl.BlockSpec(packed.shape, lambda i, *_: (0, 0))
    full = jax.ShapeDtypeStruct((row_count, columns), BF16)
    full_f32 = jax.ShapeDtypeStruct((row_count, columns), F32)

    def scores(where, key_len, query_rows, key_rows, value_rows, *keys):
        return pl.pallas_call(
            functools.partial(scores_kernel, width, levels),
            grid_spec=pltpu.PrefetchScalarGridSpec(
                num_scalar_prefetch=2,
                grid=grid,
                in_specs=[wide] * (1 + levels + 1 + 1),
                out_specs=[wide] * levels + [narrow, wide],
            ),
            out_shape=[full] * levels + [jax.ShapeDtypeStruct((row_count, grid[0] * 128), F32), full_f32],
            compiler_params=params(),
            name="scores",
        )(where, key_len, query_rows, key_rows, *keys, value_rows)

    far_keys = [moved(key_rows, turns[0])]
    keep, near, payload = fenced(block_sums, where, key_len, key_rows, value_rows)
    near_keys = moved(after(key_rows, near), swaps)
    hops = [moved(payload, steps[0])]
    far_keys += [moved(after(key_rows, near), turn) for turn in turns[1:]]
    hops.append(moved(add_packed(one, keep, after(near, far_keys[0]), *hops), steps[1]))
    held = [pair for pair in turns[0] if pair[0] < 2 and levels == 3]
    early = [pair for pair in turns[0] if pair not in held]
    first_values = [moved(after(value_rows, near_keys), early)]
    near_values = moved(after(value_rows, near_keys, *far_keys), swaps)
    if held:
        first_values.append(moved(after(value_rows, near_keys, *far_keys), held))
    far_values = [moved(after(value_rows, hops[1]), turn) for turn in turns[1:]]

    def last_hop(keep, parts, *operands):
        for pairs in steps[2:]:
            parts = [*parts, moved(add_packed(one, keep, *parts), pairs)]
        return parts[1:], scores(*operands)

    hops, (*weights, factors, base) = fenced(
        last_hop, keep, [near, *hops], where, key_len, query_rows, key_rows, value_rows, near_keys, *far_keys
    )

    far = moved(add_packed(1 - lax.rem(where, 2), keep, *hops), swaps)

    def linear(own, *parts):
        return pl.pallas_call(
            functools.partial(linear_kernel, heads, width, own, len(parts), tokens),
            in_specs=[smem, smem] + [vmem] * (1 + len(parts)),
            out_specs=vmem,
            out_shape=jax.ShapeDtypeStruct((row_count, columns // 2), F32),
            compiler_params=params(),
            name="linear_own" if own else "linear_other",
        )(where, linear_scale, query_rows, *parts)

    own = linear(True, *hops, after(near, first_values[0]))
    base, *weights[2:] = pl.pallas_call(
        functools.partial(parts_kernel, width, [1, len(first_values)], late - 1),
        grid=grid,
        in_specs=[narrow] + [wide] * (1 + 2 + 1 + len(first_values) + late - 1),
        out_specs=[wide] * late,
        out_shape=[full_f32] + [full] * (late - 1),
        compiler_params=params(),
        name="parts",
    )(factors, after(base, own), *weights[:2], near_values, *first_values, *weights[2:])

    other = linear(False, far)
    return pl.pallas_call(
        functools.partial(finish_kernel, heads, width, late, a_step),
        in_specs=[smem] + [vmem] * (4 + 2 * (late - 1)),
        out_specs=vmem,
        out_shape=full,
        compiler_params=params(),
        name="finish",
    )(where, factors, base, own, other, *weights[2:], *far_values)


def solution(mesh):
    return jax.shard_map(
        shards,
        mesh=mesh,
        in_specs=(
            P(("groups", "seq"), "head"),
            P(("groups", "seq"), "head"),
            P(("groups", "seq"), "head"),
            P("groups"),
            P("head"),
        ),
        out_specs=P(("groups", "seq"), "head"),
        check_vma=False,
    )
```

```python
import functools
import math

import jax
import jax.numpy as jnp
from jax import lax
from jax.experimental import pallas as pl
from jax.experimental.pallas import tpu as pltpu
from jax.sharding import PartitionSpec as P

CENTER = 1.125
TERMS = 2
HEADS_A_STEP = 4
VMEM_BYTES = 40 * 1024 * 1024
F32 = jnp.float32
BF16 = jnp.bfloat16


def feature(x):
    return jnp.where(x > 0.0, x + 1.0, jnp.exp(jnp.minimum(x, 0.0)))


def halves(x):
    high = x.astype(BF16)
    return high, (x - high.astype(F32)).astype(BF16)


def padded(count):
    return -(-count // 16) * 16


def store_packed(ref, main, sums):
    rows = main.shape[0]
    ref[0:rows, :] = main.astype(BF16)
    store_sums(ref, rows, sums)


def store_sums(ref, rows, sums):
    extra = sums.shape[0]
    for term in range(TERMS):
        part = sums.astype(BF16)
        sums = sums - part.astype(F32)
        ref[rows + term * extra : rows + (term + 1) * extra, :] = part


def packed_sums(ref, rows, extra):
    total = ref[rows : rows + extra, :].astype(F32)
    for term in range(1, TERMS):
        total = total + ref[rows + term * extra : rows + (term + 1) * extra, :].astype(F32)
    return total


def block_sums_kernel(heads, width, sent, where, lengths, k_ref, v_ref, out_ref):
    half_heads = heads // 2
    me = where[0]
    side = lax.rem(me, 2)
    length = lengths[me]
    rows = half_heads * width
    extra = padded(half_heads)
    first = (1 - side if sent else side) * half_heads
    live = lax.broadcasted_iota(jnp.int32, (k_ref.shape[0], width), 0) < length
    sums = []
    for i in range(half_heads):
        columns = pl.ds(pl.multiple_of((first + i) * width, width), width)
        mapped = jnp.where(live, feature(k_ref[:, columns].astype(F32)) - CENTER, 0.0)
        values = jnp.where(live, v_ref[:, columns].astype(F32), 0.0)
        sums.append(jnp.sum(values, axis=0, keepdims=True))
        high, low = halves(mapped)
        values = values.astype(BF16)
        out_ref[i * width : (i + 1) * width, :] = lax.dot_general(
            jnp.concatenate([high, low], axis=0),
            jnp.concatenate([values, values], axis=0),
            (((0,), (0,)), ((), ())),
            preferred_element_type=F32,
        ).astype(out_ref.dtype)
    sums = jnp.concatenate(sums + [jnp.zeros((1, width), F32)] * (extra - half_heads), axis=0)
    if sent:
        store_sums(out_ref, rows, sums)
    else:
        out_ref[rows : rows + extra, :] = sums


def add_packed_kernel(rows, extra, count, where, keep_ref, *refs):
    flag = where[0].astype(F32)
    main = keep_ref[0:rows, :] * flag
    sums = keep_ref[rows : rows + extra, :] * flag
    for ref in refs[:count]:
        main = main + ref[0:rows, :].astype(F32)
        sums = sums + packed_sums(ref, rows, extra)
    store_packed(refs[count], main, sums)


def partners(me, levels):
    if levels != 3:
        return [me] + [jnp.bitwise_xor(me, 1 << level) for level in range(levels)]
    pair = me // 2
    inner = lax.rem(pair + pair // 2, 2)
    return [me, jnp.bitwise_xor(me, 1), jnp.bitwise_xor(me, 2 + 2 * inner), jnp.bitwise_xor(me, 4 - 2 * inner)]


def exchanges(levels):
    count = 1 << levels
    if levels != 3:
        return [[(i, i ^ 1 << level) for i in range(count)] for level in range(1, levels)]
    cycle = [(0, 2), (2, 3), (3, 1), (1, 0)]
    return [
        [(2 * a + y, 2 * b + y) for a, b in cycle for y in (0, 1)],
        [(2 * b + y, 2 * a + y) for a, b in cycle for y in (0, 1)],
    ]


def scores_kernel(width, levels, where, lengths, q_ref, *refs):
    key_refs, refs = refs[: levels + 1], refs[levels + 1 :]
    value_ref, refs = refs[0], refs[1:]
    weight_refs, (factor_ref, base_ref) = refs[:levels], refs[levels:]
    row_count = q_ref.shape[0]
    a_step = q_ref.shape[1] // width
    column = lax.broadcasted_iota(jnp.int32, (row_count, row_count), 1)
    row = lax.broadcasted_iota(jnp.int32, (row_count, row_count), 0)
    allowed = [column < lengths[partner] for partner in partners(where[0], levels)]
    allowed[0] = allowed[0] & (column <= row)
    lane = lax.broadcasted_iota(jnp.int32, (row_count, 128), 1)
    factors = jnp.zeros((row_count, 128), F32)
    for h in range(a_step):
        at = slice(h * width, (h + 1) * width)
        queries = q_ref[:, at]
        peaks, totals, weights = [], [], []
        for which in range(levels + 1):
            s = lax.dot_general(
                queries, key_refs[which][:, at], (((1,), (1,)), ((), ())), preferred_element_type=F32
            ) * (1.0 / math.sqrt(width))
            s = jnp.where(allowed[which], s, -jnp.inf)
            peak = jnp.max(s, axis=1, keepdims=True)
            p = jnp.exp(s - peak).astype(BF16)
            peaks.append(peak)
            weights.append(p)
            totals.append(jnp.sum(p.astype(F32), axis=1, keepdims=True))
        peak = functools.reduce(jnp.maximum, peaks)
        shares = [jnp.exp(one - peak) for one in peaks]
        whole = functools.reduce(jnp.add, [a * b for a, b in zip(shares, totals)])
        shares = [share / whole for share in shares]
        base_ref[:, at] = shares[0] * jnp.dot(weights[0], value_ref[:, at], preferred_element_type=F32)
        for which in range(levels):
            weight_refs[which][:, at] = weights[which + 1]
            factors = jnp.where(lane == which * a_step + h, shares[which + 1], factors)
    factor_ref[...] = factors


def parts_kernel(width, counts, passed, factor_ref, base_ref, *refs):
    weight_refs, refs = refs[: len(counts)], refs[len(counts) :]
    last = len(refs) - 1 - 2 * passed
    value_refs, out_ref = refs[:last], refs[last + passed]
    for source, target in zip(refs[last : last + passed], refs[last + passed + 1 :]):
        target[...] = source[...]
    a_step = base_ref.shape[1] // width
    for h in range(a_step):
        at = slice(h * width, (h + 1) * width)
        total = base_ref[:, at]
        first = 0
        for which, count in enumerate(counts):
            values = functools.reduce(jnp.add, [ref[:, at] for ref in value_refs[first : first + count]])
            first += count
            lane = which * a_step + h
            total = total + factor_ref[:, lane : lane + 1] * jnp.dot(
                weight_refs[which][:, at], values, preferred_element_type=F32
            )
        out_ref[:, at] = total


def linear_kernel(heads, width, own, parts, tokens, where, scale, q_ref, *refs):
    part_refs, out_ref = refs[:parts], refs[parts]
    side = lax.rem(where[0], 2)
    half_heads = heads // 2
    rows, extra = half_heads * width, padded(half_heads)
    start = (side if own else 1 - side) * half_heads
    flags = [1.0] * (parts - 1) + [side.astype(F32) if own else 1.0]
    sums = functools.reduce(
        jnp.add, [flag * packed_sums(ref, rows, extra) for flag, ref in zip(flags, part_refs)]
    )
    for h in range(half_heads):
        at = pl.ds(pl.multiple_of((start + h) * width, width), width)
        block = slice(h * width, (h + 1) * width)
        mapped = feature(q_ref[:, at].astype(F32))
        high, low = halves(mapped)
        if own:
            prefix = functools.reduce(
                jnp.add, [flag * ref[block, :].astype(F32) for flag, ref in zip(flags, part_refs)]
            )
            prefix, rest = halves(prefix)
        else:
            prefix = part_refs[0][block, :]
        linear = jnp.dot(
            jnp.concatenate([high, low], axis=1),
            jnp.concatenate([prefix, prefix], axis=0),
            preferred_element_type=F32,
        )
        if own:
            linear = linear + jnp.dot(high, rest, preferred_element_type=F32)
        linear = linear + jnp.sum(mapped, axis=1, keepdims=True) * (CENTER * sums[h : h + 1, :])
        out_ref[:, block] = linear * (scale[start + h] * (1.0 / (width * math.sqrt(tokens))))


def finish_kernel(heads, width, late, a_step, where, factor_ref, base_ref, own_ref, other_ref, *refs):
    weight_refs, value_refs, out_ref = refs[: late - 1], refs[late - 1 : -1], refs[-1]
    step = pl.program_id(0)
    half_heads = heads // 2
    own = step == lax.rem(where[0], 2)
    for h in range(half_heads):
        block = slice(h * width, (h + 1) * width)
        at = pl.ds(pl.multiple_of((step * half_heads + h) * width, width), width)
        total = base_ref[:, at] + jnp.where(own, own_ref[:, block], other_ref[:, block])
        column = pl.ds(pl.multiple_of((step * half_heads + h) // a_step * 128, 128), 128)
        factors = factor_ref[:, column]
        for which in range(late - 1):
            lane = (which + 2) * a_step + h % a_step
            total = total + factors[:, lane : lane + 1] * jnp.dot(
                weight_refs[which][:, at], value_refs[which][:, at], preferred_element_type=F32
            )
        out_ref[:, block] = total.astype(BF16)


def params():
    return pltpu.CompilerParams(vmem_limit_bytes=VMEM_BYTES)


def shards(query_rows, key_rows, value_rows, key_len, linear_scale):
    row_count, columns = query_rows.shape
    heads = linear_scale.shape[0]
    width = columns // heads
    half_heads = heads // 2
    count = lax.axis_size("seq")
    levels = count.bit_length() - 1
    late = levels - 1
    me = lax.axis_index("seq").astype(jnp.int32)
    where = me.reshape(1)
    tokens = row_count * count
    rows, extra = half_heads * width, padded(half_heads)
    packed = jax.ShapeDtypeStruct((rows + TERMS * extra, width), BF16)
    smem = pl.BlockSpec(memory_space=pltpu.SMEM)
    vmem = pl.BlockSpec(memory_space=pltpu.VMEM)

    pairs_of_blocks = count // 2
    if pairs_of_blocks <= 4:
        steps = [[(z, z + 1)] for z in range(pairs_of_blocks - 1)]
    else:
        steps = [
            [(z, z + (1 << d)) for z in range(pairs_of_blocks - (1 << d))]
            for d in range((pairs_of_blocks - 1).bit_length())
        ]
    steps = [[(2 * a + y, 2 * b + y) for a, b in pairs for y in (0, 1)] for pairs in steps]
    swaps = [(i, i ^ 1) for i in range(count)]
    turns = exchanges(levels)

    def moved(x, pairs):
        return lax.ppermute(x, "seq", pairs)

    def after(x, *done):
        return lax.optimization_barrier((x, *done))[0]

    def fenced(run, *operands):
        shapes = jax.eval_shape(run, *operands)

        def nothing(*_):
            return jax.tree.map(lambda leaf: jnp.zeros(leaf.shape, leaf.dtype), shapes)

        return lax.cond(key_len[0] > 0, run, nothing, *operands)

    one = jnp.ones((1,), jnp.int32)

    def block_sums(where, key_len, key_rows, value_rows):
        def half(sent, shape):
            return pl.pallas_call(
                functools.partial(block_sums_kernel, heads, width, sent),
                in_specs=[smem, smem, vmem, vmem],
                out_specs=vmem,
                out_shape=shape,
                compiler_params=params(),
                name="sums_sent" if sent else "sums_kept",
            )(where, key_len, key_rows, value_rows)

        near = moved(half(True, packed), swaps)
        keep = half(False, jax.ShapeDtypeStruct((rows + extra, width), F32))
        return keep, near, add_packed(one, keep, near)

    def add_packed(flag, keep, *parts):
        return pl.pallas_call(
            functools.partial(add_packed_kernel, rows, extra, len(parts)),
            in_specs=[smem] + [vmem] * (1 + len(parts)),
            out_specs=vmem,
            out_shape=packed,
            compiler_params=params(),
            name="add_packed",
        )(flag, keep, *parts)

    a_step = math.gcd(HEADS_A_STEP, half_heads)
    grid = (heads // a_step,)
    wide = pl.BlockSpec((row_count, a_step * width), lambda i, *_: (0, i))
    narrow = pl.BlockSpec((row_count, 128), lambda i, *_: (0, i))
    whole = pl.BlockSpec(packed.shape, lambda i, *_: (0, 0))
    full = jax.ShapeDtypeStruct((row_count, columns), BF16)
    full_f32 = jax.ShapeDtypeStruct((row_count, columns), F32)

    def scores(where, key_len, query_rows, key_rows, value_rows, *keys):
        return pl.pallas_call(
            functools.partial(scores_kernel, width, levels),
            grid_spec=pltpu.PrefetchScalarGridSpec(
                num_scalar_prefetch=2,
                grid=grid,
                in_specs=[wide] * (1 + levels + 1 + 1),
                out_specs=[wide] * levels + [narrow, wide],
            ),
            out_shape=[full] * levels + [jax.ShapeDtypeStruct((row_count, grid[0] * 128), F32), full_f32],
            compiler_params=params(),
            name="scores",
        )(where, key_len, query_rows, key_rows, *keys, value_rows)

    far_keys = [moved(key_rows, turns[0])]
    keep, near, payload = fenced(block_sums, where, key_len, key_rows, value_rows)
    near_keys = moved(after(key_rows, near), swaps)
    hops = [moved(payload, steps[0])]
    far_keys += [moved(after(key_rows, near), turn) for turn in turns[1:]]
    hops.append(moved(add_packed(one, keep, after(near, far_keys[0]), *hops), steps[1]))
    held = [pair for pair in turns[0] if pair[0] < 2 and levels == 3]
    early = [pair for pair in turns[0] if pair not in held]
    first_values = [moved(after(value_rows, near_keys), early)]
    near_values = moved(after(value_rows, near_keys, *far_keys), swaps)
    if held:
        first_values.append(moved(after(value_rows, near_keys, *far_keys), held))
    far_values = [moved(after(value_rows, hops[1]), turn) for turn in turns[1:]]

    def last_hop(keep, parts, *operands):
        for pairs in steps[2:]:
            parts = [*parts, moved(add_packed(one, keep, *parts), pairs)]
        return parts[1:], scores(*operands)

    hops, (*weights, factors, base) = fenced(
        last_hop, keep, [near, *hops], where, key_len, query_rows, key_rows, value_rows, near_keys, *far_keys
    )

    far = moved(add_packed(1 - lax.rem(where, 2), keep, *hops), swaps)

    def linear(own, *parts):
        return pl.pallas_call(
            functools.partial(linear_kernel, heads, width, own, len(parts), tokens),
            in_specs=[smem, smem] + [vmem] * (1 + len(parts)),
            out_specs=vmem,
            out_shape=jax.ShapeDtypeStruct((row_count, columns // 2), F32),
            compiler_params=params(),
            name="linear_own" if own else "linear_other",
        )(where, linear_scale, query_rows, *parts)

    own = linear(True, *hops, after(near, first_values[0]))
    base, *weights[2:] = pl.pallas_call(
        functools.partial(parts_kernel, width, [1, len(first_values)], late - 1),
        grid=grid,
        in_specs=[narrow] + [wide] * (1 + 2 + 1 + len(first_values) + late - 1),
        out_specs=[wide] * late,
        out_shape=[full_f32] + [full] * (late - 1),
        compiler_params=params(),
        name="parts",
    )(factors, after(base, own), *weights[:2], near_values, *first_values, *weights[2:])

    other = linear(False, far)
    return pl.pallas_call(
        functools.partial(finish_kernel, heads, width, late, a_step),
        grid=(2,),
        in_specs=[smem] + [vmem] * (4 + 2 * (late - 1)),
        out_specs=pl.BlockSpec((row_count, columns // 2), lambda i: (0, i)),
        out_shape=full,
        compiler_params=params(),
        name="finish",
    )(where, factors, base, own, other, *weights[2:], *far_values)


def solution(mesh):
    return jax.shard_map(
        shards,
        mesh=mesh,
        in_specs=(
            P(("groups", "seq"), "head"),
            P(("groups", "seq"), "head"),
            P(("groups", "seq"), "head"),
            P("groups"),
            P("head"),
        ),
        out_specs=P(("groups", "seq"), "head"),
        check_vma=False,
    )
```

```python
import functools
import math

import jax
import jax.numpy as jnp
from jax import lax
from jax.experimental import pallas as pl
from jax.experimental.pallas import tpu as pltpu
from jax.sharding import PartitionSpec as P

CENTER = 1.125
TERMS = 2
HEADS_A_STEP = 4
VMEM_BYTES = 40 * 1024 * 1024
F32 = jnp.float32
BF16 = jnp.bfloat16


def feature(x):
    return jnp.where(x > 0.0, x + 1.0, jnp.exp(jnp.minimum(x, 0.0)))


def halves(x):
    high = x.astype(BF16)
    return high, (x - high.astype(F32)).astype(BF16)


def padded(count):
    return -(-count // 16) * 16


def store_packed(ref, main, sums):
    rows = main.shape[0]
    ref[0:rows, :] = main.astype(BF16)
    store_sums(ref, rows, sums)


def store_sums(ref, rows, sums):
    extra = sums.shape[0]
    for term in range(TERMS):
        part = sums.astype(BF16)
        sums = sums - part.astype(F32)
        ref[rows + term * extra : rows + (term + 1) * extra, :] = part


def packed_sums(ref, rows, extra):
    total = ref[rows : rows + extra, :].astype(F32)
    for term in range(1, TERMS):
        total = total + ref[rows + term * extra : rows + (term + 1) * extra, :].astype(F32)
    return total


def block_sums_kernel(heads, width, sent, where, lengths, k_ref, v_ref, out_ref):
    half_heads = heads // 2
    me = where[0]
    side = lax.rem(me, 2)
    length = lengths[me]
    rows = half_heads * width
    extra = padded(half_heads)
    first = (1 - side if sent else side) * half_heads
    live = lax.broadcasted_iota(jnp.int32, (k_ref.shape[0], width), 0) < length
    sums = []
    for i in range(half_heads):
        columns = pl.ds(pl.multiple_of((first + i) * width, width), width)
        mapped = jnp.where(live, feature(k_ref[:, columns].astype(F32)) - CENTER, 0.0)
        values = jnp.where(live, v_ref[:, columns].astype(F32), 0.0)
        sums.append(jnp.sum(values, axis=0, keepdims=True))
        high, low = halves(mapped)
        values = values.astype(BF16)
        out_ref[i * width : (i + 1) * width, :] = lax.dot_general(
            jnp.concatenate([high, low], axis=0),
            jnp.concatenate([values, values], axis=0),
            (((0,), (0,)), ((), ())),
            preferred_element_type=F32,
        ).astype(out_ref.dtype)
    sums = jnp.concatenate(sums + [jnp.zeros((1, width), F32)] * (extra - half_heads), axis=0)
    if sent:
        store_sums(out_ref, rows, sums)
    else:
        out_ref[rows : rows + extra, :] = sums


def add_packed_kernel(rows, extra, count, where, keep_ref, *refs):
    flag = where[0].astype(F32)
    main = keep_ref[0:rows, :] * flag
    sums = keep_ref[rows : rows + extra, :] * flag
    for ref in refs[:count]:
        main = main + ref[0:rows, :].astype(F32)
        sums = sums + packed_sums(ref, rows, extra)
    store_packed(refs[count], main, sums)


def partners(me, levels):
    if levels != 3:
        return [me] + [jnp.bitwise_xor(me, 1 << level) for level in range(levels)]
    pair = me // 2
    inner = lax.rem(pair + pair // 2, 2)
    return [me, jnp.bitwise_xor(me, 1), jnp.bitwise_xor(me, 2 + 2 * inner), jnp.bitwise_xor(me, 4 - 2 * inner)]


def exchanges(levels):
    count = 1 << levels
    if levels != 3:
        return [[(i, i ^ 1 << level) for i in range(count)] for level in range(1, levels)]
    cycle = [(0, 2), (2, 3), (3, 1), (1, 0)]
    return [
        [(2 * a + y, 2 * b + y) for a, b in cycle for y in (0, 1)],
        [(2 * b + y, 2 * a + y) for a, b in cycle for y in (0, 1)],
    ]


def scores_kernel(width, levels, where, lengths, q_ref, *refs):
    key_refs, refs = refs[: levels + 1], refs[levels + 1 :]
    value_ref, refs = refs[0], refs[1:]
    weight_refs, (factor_ref, base_ref) = refs[:levels], refs[levels:]
    row_count = q_ref.shape[0]
    a_step = q_ref.shape[1] // width
    column = lax.broadcasted_iota(jnp.int32, (row_count, row_count), 1)
    row = lax.broadcasted_iota(jnp.int32, (row_count, row_count), 0)
    allowed = [column < lengths[partner] for partner in partners(where[0], levels)]
    allowed[0] = allowed[0] & (column <= row)
    lane = lax.broadcasted_iota(jnp.int32, (row_count, 128), 1)
    factors = jnp.zeros((row_count, 128), F32)
    for h in range(a_step):
        at = slice(h * width, (h + 1) * width)
        queries = q_ref[:, at]
        peaks, totals, weights = [], [], []
        for which in range(levels + 1):
            s = lax.dot_general(
                queries, key_refs[which][:, at], (((1,), (1,)), ((), ())), preferred_element_type=F32
            ) * (1.0 / math.sqrt(width))
            s = jnp.where(allowed[which], s, -jnp.inf)
            peak = jnp.max(s, axis=1, keepdims=True)
            p = jnp.exp(s - peak).astype(BF16)
            peaks.append(peak)
            weights.append(p)
            totals.append(jnp.sum(p.astype(F32), axis=1, keepdims=True))
        peak = functools.reduce(jnp.maximum, peaks)
        shares = [jnp.exp(one - peak) for one in peaks]
        whole = functools.reduce(jnp.add, [a * b for a, b in zip(shares, totals)])
        shares = [share / whole for share in shares]
        base_ref[:, at] = shares[0] * jnp.dot(weights[0], value_ref[:, at], preferred_element_type=F32)
        for which in range(levels):
            weight_refs[which][:, at] = weights[which + 1]
            factors = jnp.where(lane == which * a_step + h, shares[which + 1], factors)
    factor_ref[...] = factors


def parts_kernel(width, counts, passed, factor_ref, base_ref, *refs):
    weight_refs, refs = refs[: len(counts)], refs[len(counts) :]
    last = len(refs) - 1 - 2 * passed
    value_refs, out_ref = refs[:last], refs[last + passed]
    for source, target in zip(refs[last : last + passed], refs[last + passed + 1 :]):
        target[...] = source[...]
    a_step = base_ref.shape[1] // width
    for h in range(a_step):
        at = slice(h * width, (h + 1) * width)
        total = base_ref[:, at]
        first = 0
        for which, count in enumerate(counts):
            values = functools.reduce(jnp.add, [ref[:, at] for ref in value_refs[first : first + count]])
            first += count
            lane = which * a_step + h
            total = total + factor_ref[:, lane : lane + 1] * jnp.dot(
                weight_refs[which][:, at], values, preferred_element_type=F32
            )
        out_ref[:, at] = total


def linear_kernel(heads, width, own, parts, tokens, where, scale, q_ref, *refs):
    part_refs, out_ref = refs[:parts], refs[parts]
    side = lax.rem(where[0], 2)
    half_heads = heads // 2
    rows, extra = half_heads * width, padded(half_heads)
    start = (side if own else 1 - side) * half_heads
    flags = [1.0] * (parts - 1) + [side.astype(F32) if own else 1.0]
    sums = functools.reduce(
        jnp.add, [flag * packed_sums(ref, rows, extra) for flag, ref in zip(flags, part_refs)]
    )
    for h in range(half_heads):
        at = pl.ds(pl.multiple_of((start + h) * width, width), width)
        block = slice(h * width, (h + 1) * width)
        mapped = feature(q_ref[:, at].astype(F32))
        high, low = halves(mapped)
        if own:
            prefix = functools.reduce(
                jnp.add, [flag * ref[block, :].astype(F32) for flag, ref in zip(flags, part_refs)]
            )
            prefix, rest = halves(prefix)
        else:
            prefix = part_refs[0][block, :]
        linear = jnp.dot(
            jnp.concatenate([high, low], axis=1),
            jnp.concatenate([prefix, prefix], axis=0),
            preferred_element_type=F32,
        )
        if own:
            linear = linear + jnp.dot(high, rest, preferred_element_type=F32)
        linear = linear + jnp.sum(mapped, axis=1, keepdims=True) * (CENTER * sums[h : h + 1, :])
        out_ref[:, block] = linear * (scale[start + h] * (1.0 / (width * math.sqrt(tokens))))


def join_kernel(where, base_ref, own_ref, other_ref, out_ref):
    side = lax.rem(where[0], 2)
    half = own_ref.shape[1]
    for ref, start in ((own_ref, side * half), (other_ref, (1 - side) * half)):
        at = pl.ds(pl.multiple_of(start, half), half)
        out_ref[:, at] = base_ref[:, at] + ref[...]


def finish_kernel(heads, width, late, a_step, factor_ref, base_ref, *refs):
    weight_refs, value_refs, out_ref = refs[: late - 1], refs[late - 1 : -1], refs[-1]
    step = pl.program_id(0)
    half_heads = heads // 2
    for h in range(half_heads):
        block = slice(h * width, (h + 1) * width)
        at = pl.ds(pl.multiple_of((step * half_heads + h) * width, width), width)
        total = base_ref[:, at]
        column = pl.ds(pl.multiple_of((step * half_heads + h) // a_step * 128, 128), 128)
        factors = factor_ref[:, column]
        for which in range(late - 1):
            lane = (which + 2) * a_step + h % a_step
            total = total + factors[:, lane : lane + 1] * jnp.dot(
                weight_refs[which][:, at], value_refs[which][:, at], preferred_element_type=F32
            )
        out_ref[:, block] = total.astype(BF16)


def params():
    return pltpu.CompilerParams(vmem_limit_bytes=VMEM_BYTES)


def shards(query_rows, key_rows, value_rows, key_len, linear_scale):
    row_count, columns = query_rows.shape
    heads = linear_scale.shape[0]
    width = columns // heads
    half_heads = heads // 2
    count = lax.axis_size("seq")
    levels = count.bit_length() - 1
    late = levels - 1
    me = lax.axis_index("seq").astype(jnp.int32)
    where = me.reshape(1)
    tokens = row_count * count
    rows, extra = half_heads * width, padded(half_heads)
    packed = jax.ShapeDtypeStruct((rows + TERMS * extra, width), BF16)
    smem = pl.BlockSpec(memory_space=pltpu.SMEM)
    vmem = pl.BlockSpec(memory_space=pltpu.VMEM)

    pairs_of_blocks = count // 2
    if pairs_of_blocks <= 4:
        steps = [[(z, z + 1)] for z in range(pairs_of_blocks - 1)]
    else:
        steps = [
            [(z, z + (1 << d)) for z in range(pairs_of_blocks - (1 << d))]
            for d in range((pairs_of_blocks - 1).bit_length())
        ]
    steps = [[(2 * a + y, 2 * b + y) for a, b in pairs for y in (0, 1)] for pairs in steps]
    swaps = [(i, i ^ 1) for i in range(count)]
    turns = exchanges(levels)

    def moved(x, pairs):
        return lax.ppermute(x, "seq", pairs)

    def after(x, *done):
        return lax.optimization_barrier((x, *done))[0]

    def fenced(run, *operands):
        shapes = jax.eval_shape(run, *operands)

        def nothing(*_):
            return jax.tree.map(lambda leaf: jnp.zeros(leaf.shape, leaf.dtype), shapes)

        return lax.cond(key_len[0] > 0, run, nothing, *operands)

    one = jnp.ones((1,), jnp.int32)

    def block_sums(where, key_len, key_rows, value_rows):
        def half(sent, shape):
            return pl.pallas_call(
                functools.partial(block_sums_kernel, heads, width, sent),
                in_specs=[smem, smem, vmem, vmem],
                out_specs=vmem,
                out_shape=shape,
                compiler_params=params(),
                name="sums_sent" if sent else "sums_kept",
            )(where, key_len, key_rows, value_rows)

        near = moved(half(True, packed), swaps)
        keep = half(False, jax.ShapeDtypeStruct((rows + extra, width), F32))
        return keep, near, add_packed(one, keep, near)

    def add_packed(flag, keep, *parts):
        return pl.pallas_call(
            functools.partial(add_packed_kernel, rows, extra, len(parts)),
            in_specs=[smem] + [vmem] * (1 + len(parts)),
            out_specs=vmem,
            out_shape=packed,
            compiler_params=params(),
            name="add_packed",
        )(flag, keep, *parts)

    a_step = math.gcd(HEADS_A_STEP, half_heads)
    grid = (heads // a_step,)
    wide = pl.BlockSpec((row_count, a_step * width), lambda i, *_: (0, i))
    narrow = pl.BlockSpec((row_count, 128), lambda i, *_: (0, i))
    whole = pl.BlockSpec(packed.shape, lambda i, *_: (0, 0))
    full = jax.ShapeDtypeStruct((row_count, columns), BF16)
    full_f32 = jax.ShapeDtypeStruct((row_count, columns), F32)

    def scores(where, key_len, query_rows, key_rows, value_rows, *keys):
        return pl.pallas_call(
            functools.partial(scores_kernel, width, levels),
            grid_spec=pltpu.PrefetchScalarGridSpec(
                num_scalar_prefetch=2,
                grid=grid,
                in_specs=[wide] * (1 + levels + 1 + 1),
                out_specs=[wide] * levels + [narrow, wide],
            ),
            out_shape=[full] * levels + [jax.ShapeDtypeStruct((row_count, grid[0] * 128), F32), full_f32],
            compiler_params=params(),
            name="scores",
        )(where, key_len, query_rows, key_rows, *keys, value_rows)

    far_keys = [moved(key_rows, turns[0])]
    keep, near, payload = fenced(block_sums, where, key_len, key_rows, value_rows)
    near_keys = moved(after(key_rows, near), swaps)
    hops = [moved(payload, steps[0])]
    far_keys += [moved(after(key_rows, near), turn) for turn in turns[1:]]
    hops.append(moved(add_packed(one, keep, after(near, far_keys[0]), *hops), steps[1]))
    held = [pair for pair in turns[0] if pair[0] < 2 and levels == 3]
    early = [pair for pair in turns[0] if pair not in held]
    first_values = [moved(after(value_rows, near_keys), early)]
    near_values = moved(after(value_rows, near_keys, *far_keys), swaps)
    if held:
        first_values.append(moved(after(value_rows, near_keys, *far_keys), held))
    far_values = [moved(after(value_rows, hops[1]), turn) for turn in turns[1:]]

    def last_hop(keep, parts, *operands):
        for pairs in steps[2:]:
            parts = [*parts, moved(add_packed(one, keep, *parts), pairs)]
        return parts[1:], scores(*operands)

    hops, (*weights, factors, base) = fenced(
        last_hop, keep, [near, *hops], where, key_len, query_rows, key_rows, value_rows, near_keys, *far_keys
    )

    far = moved(add_packed(1 - lax.rem(where, 2), keep, *hops), swaps)

    def linear(own, *parts):
        return pl.pallas_call(
            functools.partial(linear_kernel, heads, width, own, len(parts), tokens),
            in_specs=[smem, smem] + [vmem] * (1 + len(parts)),
            out_specs=vmem,
            out_shape=jax.ShapeDtypeStruct((row_count, columns // 2), F32),
            compiler_params=params(),
            name="linear_own" if own else "linear_other",
        )(where, linear_scale, query_rows, *parts)

    own = linear(True, *hops, after(near, first_values[0]))
    base, *weights[2:] = pl.pallas_call(
        functools.partial(parts_kernel, width, [1, len(first_values)], late - 1),
        grid=grid,
        in_specs=[narrow] + [wide] * (1 + 2 + 1 + len(first_values) + late - 1),
        out_specs=[wide] * late,
        out_shape=[full_f32] + [full] * (late - 1),
        compiler_params=params(),
        name="parts",
    )(factors, after(base, own), *weights[:2], near_values, *first_values, *weights[2:])

    other = linear(False, far)
    base = pl.pallas_call(
        join_kernel,
        in_specs=[smem] + [vmem] * 3,
        out_specs=vmem,
        out_shape=full_f32,
        compiler_params=params(),
        name="join",
    )(where, base, own, other)
    return pl.pallas_call(
        functools.partial(finish_kernel, heads, width, late, a_step),
        grid=(2,),
        in_specs=[vmem] * (2 + 2 * (late - 1)),
        out_specs=pl.BlockSpec((row_count, columns // 2), lambda i: (0, i)),
        out_shape=full,
        compiler_params=params(),
        name="finish",
    )(factors, base, *weights[2:], *far_values)


def solution(mesh):
    return jax.shard_map(
        shards,
        mesh=mesh,
        in_specs=(
            P(("groups", "seq"), "head"),
            P(("groups", "seq"), "head"),
            P(("groups", "seq"), "head"),
            P("groups"),
            P("head"),
        ),
        out_specs=P(("groups", "seq"), "head"),
        check_vma=False,
    )
```

```python
import functools
import math

import jax
import jax.numpy as jnp
from jax import lax
from jax.experimental import pallas as pl
from jax.experimental.pallas import tpu as pltpu
from jax.sharding import PartitionSpec as P

CENTER = 1.125
TERMS = 2
HEADS_A_STEP = 4
VMEM_BYTES = 40 * 1024 * 1024
F32 = jnp.float32
BF16 = jnp.bfloat16


def feature(x):
    return jnp.where(x > 0.0, x + 1.0, jnp.exp(jnp.minimum(x, 0.0)))


def halves(x):
    high = x.astype(BF16)
    return high, (x - high.astype(F32)).astype(BF16)


def padded(count):
    return -(-count // 16) * 16


def store_packed(ref, main, sums):
    rows = main.shape[0]
    ref[0:rows, :] = main.astype(BF16)
    store_sums(ref, rows, sums)


def store_sums(ref, rows, sums):
    extra = sums.shape[0]
    for term in range(TERMS):
        part = sums.astype(BF16)
        sums = sums - part.astype(F32)
        ref[rows + term * extra : rows + (term + 1) * extra, :] = part


def packed_sums(ref, rows, extra):
    total = ref[rows : rows + extra, :].astype(F32)
    for term in range(1, TERMS):
        total = total + ref[rows + term * extra : rows + (term + 1) * extra, :].astype(F32)
    return total


def block_sums_kernel(heads, width, sent, where, lengths, k_ref, v_ref, out_ref):
    half_heads = heads // 2
    me = where[0]
    side = lax.rem(me, 2)
    length = lengths[me]
    rows = half_heads * width
    extra = padded(half_heads)
    first = (1 - side if sent else side) * half_heads
    live = lax.broadcasted_iota(jnp.int32, (k_ref.shape[0], width), 0) < length
    sums = []
    for i in range(half_heads):
        columns = pl.ds(pl.multiple_of((first + i) * width, width), width)
        mapped = jnp.where(live, feature(k_ref[:, columns].astype(F32)) - CENTER, 0.0)
        values = jnp.where(live, v_ref[:, columns].astype(F32), 0.0)
        sums.append(jnp.sum(values, axis=0, keepdims=True))
        high, low = halves(mapped)
        values = values.astype(BF16)
        out_ref[i * width : (i + 1) * width, :] = lax.dot_general(
            jnp.concatenate([high, low], axis=0),
            jnp.concatenate([values, values], axis=0),
            (((0,), (0,)), ((), ())),
            preferred_element_type=F32,
        ).astype(out_ref.dtype)
    sums = jnp.concatenate(sums + [jnp.zeros((1, width), F32)] * (extra - half_heads), axis=0)
    if sent:
        store_sums(out_ref, rows, sums)
    else:
        out_ref[rows : rows + extra, :] = sums


def add_packed_kernel(rows, extra, count, where, keep_ref, *refs):
    flag = where[0].astype(F32)
    main = keep_ref[0:rows, :] * flag
    sums = keep_ref[rows : rows + extra, :] * flag
    for ref in refs[:count]:
        main = main + ref[0:rows, :].astype(F32)
        sums = sums + packed_sums(ref, rows, extra)
    store_packed(refs[count], main, sums)


def partners(me, levels):
    if levels != 3:
        return [me] + [jnp.bitwise_xor(me, 1 << level) for level in range(levels)]
    pair = me // 2
    inner = lax.rem(pair + pair // 2, 2)
    return [me, jnp.bitwise_xor(me, 1), jnp.bitwise_xor(me, 2 + 2 * inner), jnp.bitwise_xor(me, 4 - 2 * inner)]


def exchanges(levels):
    count = 1 << levels
    if levels != 3:
        return [[(i, i ^ 1 << level) for i in range(count)] for level in range(1, levels)]
    cycle = [(0, 2), (2, 3), (3, 1), (1, 0)]
    return [
        [(2 * a + y, 2 * b + y) for a, b in cycle for y in (0, 1)],
        [(2 * b + y, 2 * a + y) for a, b in cycle for y in (0, 1)],
    ]


def scores_kernel(width, levels, where, lengths, q_ref, *refs):
    key_refs, refs = refs[: levels + 1], refs[levels + 1 :]
    value_ref, refs = refs[0], refs[1:]
    weight_refs, (factor_ref, base_ref) = refs[:levels], refs[levels:]
    row_count = q_ref.shape[0]
    a_step = q_ref.shape[1] // width
    column = lax.broadcasted_iota(jnp.int32, (row_count, row_count), 1)
    row = lax.broadcasted_iota(jnp.int32, (row_count, row_count), 0)
    allowed = [column < lengths[partner] for partner in partners(where[0], levels)]
    allowed[0] = allowed[0] & (column <= row)
    lane = lax.broadcasted_iota(jnp.int32, (row_count, 128), 1)
    factors = jnp.zeros((row_count, 128), F32)
    for h in range(a_step):
        at = slice(h * width, (h + 1) * width)
        queries = q_ref[:, at]
        peaks, totals, weights = [], [], []
        for which in range(levels + 1):
            s = lax.dot_general(
                queries, key_refs[which][:, at], (((1,), (1,)), ((), ())), preferred_element_type=F32
            ) * (1.0 / math.sqrt(width))
            s = jnp.where(allowed[which], s, -jnp.inf)
            peak = jnp.max(s, axis=1, keepdims=True)
            p = jnp.exp(s - peak).astype(BF16)
            peaks.append(peak)
            weights.append(p)
            totals.append(jnp.sum(p.astype(F32), axis=1, keepdims=True))
        peak = functools.reduce(jnp.maximum, peaks)
        shares = [jnp.exp(one - peak) for one in peaks]
        whole = functools.reduce(jnp.add, [a * b for a, b in zip(shares, totals)])
        shares = [share / whole for share in shares]
        base_ref[:, at] = shares[0] * jnp.dot(weights[0], value_ref[:, at], preferred_element_type=F32)
        for which in range(levels):
            weight_refs[which][:, at] = weights[which + 1]
            factors = jnp.where(lane == which * a_step + h, shares[which + 1], factors)
    factor_ref[...] = factors


def parts_kernel(width, counts, passed, factor_ref, base_ref, *refs):
    weight_refs, refs = refs[: len(counts)], refs[len(counts) :]
    last = len(refs) - 1 - 2 * passed
    value_refs, out_ref = refs[:last], refs[last + passed]
    for source, target in zip(refs[last : last + passed], refs[last + passed + 1 :]):
        target[...] = source[...]
    a_step = base_ref.shape[1] // width
    for h in range(a_step):
        at = slice(h * width, (h + 1) * width)
        total = base_ref[:, at]
        first = 0
        for which, count in enumerate(counts):
            values = functools.reduce(jnp.add, [ref[:, at] for ref in value_refs[first : first + count]])
            first += count
            lane = which * a_step + h
            total = total + factor_ref[:, lane : lane + 1] * jnp.dot(
                weight_refs[which][:, at], values, preferred_element_type=F32
            )
        out_ref[:, at] = total


def linear_kernel(heads, width, own, parts, tokens, where, scale, q_ref, *refs):
    part_refs, out_ref = refs[:parts], refs[parts]
    side = lax.rem(where[0], 2)
    half_heads = heads // 2
    rows, extra = half_heads * width, padded(half_heads)
    start = (side if own else 1 - side) * half_heads
    flags = [1.0] * (parts - 1) + [side.astype(F32) if own else 1.0]
    sums = functools.reduce(
        jnp.add, [flag * packed_sums(ref, rows, extra) for flag, ref in zip(flags, part_refs)]
    )
    for h in range(half_heads):
        at = pl.ds(pl.multiple_of((start + h) * width, width), width)
        block = slice(h * width, (h + 1) * width)
        mapped = feature(q_ref[:, at].astype(F32))
        high, low = halves(mapped)
        if own:
            prefix = functools.reduce(
                jnp.add, [flag * ref[block, :].astype(F32) for flag, ref in zip(flags, part_refs)]
            )
            prefix, rest = halves(prefix)
        else:
            prefix = part_refs[0][block, :]
        linear = jnp.dot(
            jnp.concatenate([high, low], axis=1),
            jnp.concatenate([prefix, prefix], axis=0),
            preferred_element_type=F32,
        )
        if own:
            linear = linear + jnp.dot(high, rest, preferred_element_type=F32)
        linear = linear + jnp.sum(mapped, axis=1, keepdims=True) * (CENTER * sums[h : h + 1, :])
        out_ref[:, block] = linear * (scale[start + h] * (1.0 / (width * math.sqrt(tokens))))


def finish_kernel(heads, width, late, a_step, where, factor_ref, base_ref, own_ref, other_ref, *refs):
    weight_refs, value_refs, out_ref = refs[: late - 1], refs[late - 1 : -1], refs[-1]
    side = lax.rem(where[0], 2)
    half_heads = heads // 2
    for own, linear_ref in ((True, own_ref), (False, other_ref)):
        start = (side if own else 1 - side) * half_heads
        for h in range(half_heads):
            at = pl.ds(pl.multiple_of((start + h) * width, width), width)
            total = base_ref[:, at] + linear_ref[:, h * width : (h + 1) * width]
            column = pl.ds(pl.multiple_of((start + h) // a_step * 128, 128), 128)
            factors = factor_ref[:, column]
            for which in range(late - 1):
                lane = (which + 2) * a_step + h % a_step
                total = total + factors[:, lane : lane + 1] * jnp.dot(
                    weight_refs[which][:, at], value_refs[which][:, at], preferred_element_type=F32
                )
            out_ref[:, at] = total.astype(BF16)


def params():
    return pltpu.CompilerParams(vmem_limit_bytes=VMEM_BYTES)


def shards(query_rows, key_rows, value_rows, key_len, linear_scale):
    row_count, columns = query_rows.shape
    heads = linear_scale.shape[0]
    width = columns // heads
    half_heads = heads // 2
    count = lax.axis_size("seq")
    levels = count.bit_length() - 1
    late = levels - 1
    me = lax.axis_index("seq").astype(jnp.int32)
    where = me.reshape(1)
    tokens = row_count * count
    rows, extra = half_heads * width, padded(half_heads)
    packed = jax.ShapeDtypeStruct((rows + TERMS * extra, width), BF16)
    smem = pl.BlockSpec(memory_space=pltpu.SMEM)
    vmem = pl.BlockSpec(memory_space=pltpu.VMEM)

    pairs_of_blocks = count // 2
    if pairs_of_blocks <= 4:
        steps = [[(z, z + 1)] for z in range(pairs_of_blocks - 1)]
    else:
        steps = [
            [(z, z + (1 << d)) for z in range(pairs_of_blocks - (1 << d))]
            for d in range((pairs_of_blocks - 1).bit_length())
        ]
    steps = [[(2 * a + y, 2 * b + y) for a, b in pairs for y in (0, 1)] for pairs in steps]
    swaps = [(i, i ^ 1) for i in range(count)]
    turns = exchanges(levels)

    def moved(x, pairs):
        return lax.ppermute(x, "seq", pairs)

    def after(x, *done):
        return lax.optimization_barrier((x, *done))[0]

    def fenced(run, *operands):
        shapes = jax.eval_shape(run, *operands)

        def nothing(*_):
            return jax.tree.map(lambda leaf: jnp.zeros(leaf.shape, leaf.dtype), shapes)

        return lax.cond(key_len[0] > 0, run, nothing, *operands)

    one = jnp.ones((1,), jnp.int32)

    def block_sums(where, key_len, key_rows, value_rows):
        def half(sent, shape):
            return pl.pallas_call(
                functools.partial(block_sums_kernel, heads, width, sent),
                in_specs=[smem, smem, vmem, vmem],
                out_specs=vmem,
                out_shape=shape,
                compiler_params=params(),
                name="sums_sent" if sent else "sums_kept",
            )(where, key_len, key_rows, value_rows)

        near = moved(half(True, packed), swaps)
        keep = half(False, jax.ShapeDtypeStruct((rows + extra, width), F32))
        return keep, near, add_packed(one, keep, near)

    def add_packed(flag, keep, *parts):
        return pl.pallas_call(
            functools.partial(add_packed_kernel, rows, extra, len(parts)),
            in_specs=[smem] + [vmem] * (1 + len(parts)),
            out_specs=vmem,
            out_shape=packed,
            compiler_params=params(),
            name="add_packed",
        )(flag, keep, *parts)

    a_step = math.gcd(HEADS_A_STEP, half_heads)
    grid = (heads // a_step,)
    wide = pl.BlockSpec((row_count, a_step * width), lambda i, *_: (0, i))
    narrow = pl.BlockSpec((row_count, 128), lambda i, *_: (0, i))
    whole = pl.BlockSpec(packed.shape, lambda i, *_: (0, 0))
    full = jax.ShapeDtypeStruct((row_count, columns), BF16)
    full_f32 = jax.ShapeDtypeStruct((row_count, columns), F32)

    def scores(where, key_len, query_rows, key_rows, value_rows, *keys):
        return pl.pallas_call(
            functools.partial(scores_kernel, width, levels),
            grid_spec=pltpu.PrefetchScalarGridSpec(
                num_scalar_prefetch=2,
                grid=grid,
                in_specs=[wide] * (1 + levels + 1 + 1),
                out_specs=[wide] * levels + [narrow, wide],
            ),
            out_shape=[full] * levels + [jax.ShapeDtypeStruct((row_count, grid[0] * 128), F32), full_f32],
            compiler_params=params(),
            name="scores",
        )(where, key_len, query_rows, key_rows, *keys, value_rows)

    far_keys = [moved(key_rows, turns[0])]
    keep, near, payload = fenced(block_sums, where, key_len, key_rows, value_rows)
    near_keys = moved(after(key_rows, near), swaps)
    hops = [moved(payload, steps[0])]
    far_keys += [moved(after(key_rows, near), turn) for turn in turns[1:]]
    hops.append(moved(add_packed(one, keep, after(near, far_keys[0]), *hops), steps[1]))
    held = [pair for pair in turns[0] if pair[0] < 2 and levels == 3]
    early = [pair for pair in turns[0] if pair not in held]
    first_values = [moved(after(value_rows, near_keys), early)]
    near_values = moved(after(value_rows, near_keys, *far_keys), swaps)
    if held:
        first_values.append(moved(after(value_rows, near_keys, *far_keys), held))
    far_values = [moved(after(value_rows, hops[1]), turn) for turn in turns[1:]]

    def last_hop(keep, parts, *operands):
        for pairs in steps[2:]:
            parts = [*parts, moved(add_packed(one, keep, *parts), pairs)]
        return parts[1:], scores(*operands)

    hops, (*weights, factors, base) = fenced(
        last_hop, keep, [near, *hops], where, key_len, query_rows, key_rows, value_rows, near_keys, *far_keys
    )

    far = moved(add_packed(1 - lax.rem(where, 2), keep, *hops), swaps)

    def linear(own, *parts):
        return pl.pallas_call(
            functools.partial(linear_kernel, heads, width, own, len(parts), tokens),
            in_specs=[smem, smem] + [vmem] * (1 + len(parts)),
            out_specs=vmem,
            out_shape=jax.ShapeDtypeStruct((row_count, columns // 2), F32),
            compiler_params=params(),
            name="linear_own" if own else "linear_other",
        )(where, linear_scale, query_rows, *parts)

    own = linear(True, *hops, after(near, first_values[0]))
    base, *weights[2:] = pl.pallas_call(
        functools.partial(parts_kernel, width, [1, len(first_values)], late - 1),
        grid=grid,
        in_specs=[narrow] + [wide] * (1 + 2 + 1 + len(first_values) + late - 1),
        out_specs=[wide] * late,
        out_shape=[full_f32] + [full] * (late - 1),
        compiler_params=params(),
        name="parts",
    )(factors, after(base, own), *weights[:2], near_values, *first_values, *weights[2:])

    other = linear(False, far)
    return pl.pallas_call(
        functools.partial(finish_kernel, heads, width, late, a_step),
        in_specs=[smem] + [vmem] * (4 + 2 * (late - 1)),
        out_specs=vmem,
        out_shape=full,
        compiler_params=params(),
        name="finish",
    )(where, factors, base, own, other, *weights[2:], *far_values)


def solution(mesh):
    return jax.shard_map(
        shards,
        mesh=mesh,
        in_specs=(
            P(("groups", "seq"), "head"),
            P(("groups", "seq"), "head"),
            P(("groups", "seq"), "head"),
            P("groups"),
            P("head"),
        ),
        out_specs=P(("groups", "seq"), "head"),
        check_vma=False,
    )
```
